256 devices in a mesh: dp: 16 (over z, core), tensor: 16 (over y, x).
Axes of the slice: x: 4, y: 4, z: 8, core: 2. Of those that a mesh axis runs over, the one named last changes fastest.
Arguments:
- questions: bfloat16 [16, 32, 4096], P('dp', None, 'tensor'), may hold values from -30 to 30
- memory: bfloat16 [256, 128, 4096], P('dp', None, 'tensor'), may hold values from -30 to 30
- retrieved: int32 [16, 14], P('dp'), may hold values from 0 to 255, as said below
- location: int32 [256], replicated, may hold values from 0 to 255, as said below
- norm_gain: float32 [4096], replicated, may hold values from 0.1 to 1.9
- w_query: bfloat16 [4096, 4096], P(None, 'tensor'), may hold values from -0.75 to 0.75
- w_key: bfloat16 [4096, 4096], P(None, 'tensor'), may hold values from -0.75 to 0.75
- w_value: bfloat16 [4096, 4096], P(None, 'tensor'), may hold values from -0.09375 to 0.09375
- w_out: bfloat16 [4096, 4096], P('tensor'), may hold values from -0.125 to 0.125
Outputs:
- updated: bfloat16 [16, 14, 32, 4096], P('dp', None, None, 'tensor')
The draws below stay inside these ranges and needn't reach their ends.
Inputs may be any that keep to these rules, and one draw needn't show every extreme that they name: A permutation: passage p is held in row location[p] of memory, on dp index location[p] // 16. `retrieved`: the 14 passages named by the questions of one dp index are distinct; at most 2 of them are held by one dp index, and exactly 2 by some dp index.
All inputs are finite; a program needn't handle non-finite values.
Results may differ from the reference program's by a relative error of at most 0.009.
Values may be sent and summed in bfloat16 or wider, within the bound.
A program may use at most 128 MiB of HBM per device.

```python
import math
import jax
import jax.numpy as jnp
from jax import lax

D = 4096
HEADS = 64
HEAD_DIM = 64
QLEN = 32
MLEN = 128
RETRIEVED = 14
CAP = 2
Q_DEV = 1
PASS_DEV = 16
QUESTIONS = 16
PASSAGES = 256
SEQ = 160
N_TENSOR = 16


def spread(key, shape):
    return jnp.exp(jax.random.uniform(key, shape, jnp.float32, 0.0, 0.5 * math.log(10.0)))


def column_profile(key, rise):
    position = jnp.arange(D, dtype=jnp.float32) / (D - 1)
    ramp = jnp.exp(math.log(rise) * position)
    jitter = jnp.exp(jax.random.uniform(key, (D,), jnp.float32, 0.0, 0.25 * math.log(10.0)))
    return ramp * jitter


def storage(key):
    return jax.random.permutation(jax.random.fold_in(key, 101), PASSAGES).astype(jnp.int32)


def draw_location(key, part):
    return storage(key)


def draw_retrieved(key, part):
    placed = storage(key)
    key = jax.random.fold_in(key, 2)
    owners = PASSAGES // PASS_DEV
    request_count = Q_DEV * RETRIEVED
    others = owners - 1
    inverse = jnp.zeros((PASSAGES,), jnp.int32).at[placed].set(jnp.arange(PASSAGES, dtype=jnp.int32))
    key_pop, key_first, key_second, key_order, key_start, key_shuffle = jax.random.split(key, 6)
    popular = jax.random.permutation(key_pop, owners).astype(jnp.int32)
    pick_first = jnp.minimum(jax.random.randint(key_first, (owners,), 0, owners), jax.random.randint(key_second, (owners,), 0, owners))
    first_owner = popular[pick_first]
    owner_ids = jnp.arange(owners, dtype=jnp.int32)
    ranking = jax.random.randint(key_order, (owners, owners), 0, 1 << 20) * owners + owner_ids[None, :]
    ranking = jnp.where(owner_ids[None, :] == first_owner[:, None], jnp.int32(1 << 30), ranking)
    visit_order = jnp.argsort(ranking, axis=1).astype(jnp.int32)
    request_ids = jnp.arange(request_count, dtype=jnp.int32)
    beyond_first = jnp.maximum(request_ids - CAP, 0)
    other_owner = visit_order[:, beyond_first % others]
    owner_of = jnp.where(request_ids[None, :] < CAP, first_owner[:, None], other_owner)
    repeat_index = jnp.where(request_ids < CAP, request_ids, beyond_first // others)
    slot_start_draw = jax.random.randint(key_start, (owners, owners), 0, PASS_DEV)
    start_slot = jnp.take_along_axis(slot_start_draw, owner_of, axis=1)
    within = (start_slot + repeat_index[None, :]) % PASS_DEV
    storage_row = owner_of * PASS_DEV + within
    passage_ids = inverse[storage_row]
    shuffle = jnp.argsort(jax.random.randint(key_shuffle, (owners, request_count), 0, 1 << 20) * request_count + request_ids[None, :], axis=1)
    passage_ids = jnp.take_along_axis(passage_ids, shuffle, axis=1)
    return passage_ids.reshape(QUESTIONS, RETRIEVED).astype(jnp.int32)


def draw_questions(key, part):
    key = jax.random.fold_in(key, 4)
    key_rows, key_columns, key_main = jax.random.split(key, 3)
    row_scales = spread(key_rows, (QUESTIONS, QLEN, 1))
    column_scales = column_profile(key_columns, 3.0)
    entries = jax.random.normal(key_main, (QUESTIONS, QLEN, D), jnp.float32)
    return jnp.clip(0.5 * entries * row_scales * column_scales, -30.0, 30.0).astype(jnp.bfloat16)


def draw_memory(key, part):
    key = jax.random.fold_in(key, 5)
    key_rows, key_columns, key_main = jax.random.split(key, 3)
    row_scales = spread(key_rows, (PASSAGES, MLEN, 1))
    column_scales = column_profile(key_columns, 3.0)
    entries = jax.random.normal(key_main, (PASSAGES, MLEN, D), jnp.float32)
    return jnp.clip(0.5 * entries * row_scales * column_scales, -30.0, 30.0).astype(jnp.bfloat16)


def draw_w_query(key, part):
    key = jax.random.fold_in(key, 1)
    own_draw = jax.random.normal(key, (D, HEADS * HEAD_DIM), jnp.float32)
    entries = own_draw / math.sqrt(D)
    return jnp.clip(entries, -0.75, 0.75).astype(jnp.bfloat16)


def draw_w_key(key, part):
    key = jax.random.fold_in(key, 3)
    own_draw = jax.random.normal(key, (D, HEADS * HEAD_DIM), jnp.float32)
    entries = own_draw / math.sqrt(D)
    return jnp.clip(entries, -0.75, 0.75).astype(jnp.bfloat16)


def with_spikes(values, rng, source, target, blocks, factor):
    def block_of(axis_at):
        return (jnp.arange(values.shape[axis_at]) // (values.shape[axis_at] // blocks)).reshape((-1,) + (1,) * (values.ndim - 1 - axis_at))

    first = jax.random.permutation(rng, blocks)[block_of(target)]
    other_side = (block_of(target) + blocks // 2) % blocks
    return jnp.where((block_of(source) == first) | (block_of(source) == other_side), factor * values, values)


def block_scale(stream_key, shape, cuts, low, largest):
    def one(dim, blocks):
        draws = jax.random.uniform(jax.random.fold_in(jax.random.fold_in(stream_key, 6), dim), (blocks,), jnp.float32, low / len(cuts), largest / len(cuts))
        return jnp.repeat(jnp.exp(draws), shape[dim] // blocks).reshape((-1,) + (1,) * (len(shape) - dim - 1))

    loudness = one(*cuts[0])
    for cut in cuts[1:]:
        loudness = loudness * one(*cut)
    return loudness


def normal_values(stream_key, shape, width, most, cuts=(), kind=jnp.bfloat16):
    values = width * jax.random.normal(stream_key, shape, jnp.float32)
    if cuts:
        values = values * block_scale(stream_key, shape, cuts, -0.22, 0.18)
    return jnp.clip(values, -most, most).astype(kind)


def gaussian_with(key, extent, deviation, reach, cuts, heavy, kind=jnp.bfloat16):
    values = deviation * jax.random.normal(key, extent, jnp.float32)
    if cuts:
        values = values * block_scale(key, extent, cuts, -0.22, 0.18)
    return jnp.clip(with_spikes(values, jax.random.fold_in(key, 3), *heavy), -reach, reach).astype(kind)


def setup_inputs(seed: int = 0) -> dict:
    key_list = jax.random.split(jax.random.key(seed), 10)
    return {
        "questions": draw_questions(jax.random.fold_in(key_list[9], 71), 0),
        "memory": draw_memory(jax.random.fold_in(key_list[9], 71), 0),
        "retrieved": draw_retrieved(jax.random.fold_in(key_list[9], 71), 0),
        "location": draw_location(jax.random.fold_in(key_list[9], 71), 0),
        "norm_gain": jnp.clip(1.0 + 0.18 * jax.random.normal(key_list[4], (D,), jnp.float32), 0.1, 1.9),
        "w_query": draw_w_query(jax.random.fold_in(key_list[9], 71), 0),
        "w_key": draw_w_key(jax.random.fold_in(key_list[9], 71), 0),
        "w_value": normal_values(key_list[7], (D, HEADS * HEAD_DIM), D ** -0.5, 0.09375, ((1, 16),)),
        "w_out": gaussian_with(key_list[8], (HEADS * HEAD_DIM, D), (HEADS * HEAD_DIM) ** -0.5, 0.125, ((0, 16),), (0, 1, 16, 2.0)),
    }


epsilon = 1e-06

def reference(questions, memory, retrieved, location, norm_gain, w_query, w_key, w_value, w_out):
    full_width = HEADS * HEAD_DIM
    group_width = full_width // N_TENSOR

    def one_question(entry):
        tokens, picked_ids = entry
        fetched = memory[location[picked_ids]]
        stacked = jnp.concatenate([jnp.broadcast_to(tokens[None], (RETRIEVED, QLEN, D)), fetched], axis=1)
        widened = stacked.astype(jnp.float32)
        row_scale = lax.rsqrt(lax.optimization_barrier(jnp.mean(widened * widened, axis=-1, keepdims=True)) + epsilon)
        normed = (widened * norm_gain).astype(jnp.bfloat16)
        flattened = normed.reshape(RETRIEVED * SEQ, D)
        key_rows = (jnp.dot(flattened, w_key, preferred_element_type=jnp.float32).reshape(RETRIEVED, SEQ, full_width) * row_scale).astype(jnp.bfloat16)
        value_rows = (jnp.dot(flattened, w_value, preferred_element_type=jnp.float32).reshape(RETRIEVED, SEQ, full_width) * row_scale).astype(jnp.bfloat16)
        asked = normed[:, :QLEN].reshape(RETRIEVED * QLEN, D)
        query_rows = (jnp.dot(asked, w_query, preferred_element_type=jnp.float32).reshape(RETRIEVED, QLEN, full_width) * row_scale[:, :QLEN]).astype(jnp.bfloat16)
        query_four = query_rows.astype(jnp.float32).reshape(RETRIEVED, QLEN, HEADS, HEAD_DIM)
        key_four = key_rows.astype(jnp.float32).reshape(RETRIEVED, SEQ, HEADS, HEAD_DIM)
        value_four = value_rows.astype(jnp.float32).reshape(RETRIEVED, SEQ, HEADS, HEAD_DIM)
        scores = jnp.einsum('kthd,kshd->khts', query_four, key_four) * HEAD_DIM ** (-0.5)
        attention = jax.nn.softmax(scores, axis=-1).astype(jnp.bfloat16)
        context = jnp.einsum('khts,kshd->kthd', attention.astype(jnp.float32), value_four).astype(jnp.bfloat16)
        context = context.reshape(RETRIEVED * QLEN, full_width)
        summed = jnp.zeros((RETRIEVED * QLEN, D), jnp.float32)
        for group in range(N_TENSOR):
            term = jnp.dot(context[:, group * group_width:(group + 1) * group_width], w_out[group * group_width:(group + 1) * group_width], preferred_element_type=jnp.float32)
            rounded = lax.optimization_barrier(term.astype(jnp.bfloat16))
            summed = summed + rounded.astype(jnp.float32)
        result = tokens.astype(jnp.float32)[None] + summed.reshape(RETRIEVED, QLEN, D)
        return result.astype(jnp.bfloat16)
    return lax.map(one_question, (questions, retrieved))
```

```python
import functools

import jax
import jax.numpy as jnp
from jax import lax
from jax.experimental import pallas as pl
from jax.experimental.pallas import tpu as pltpu
from jax.sharding import PartitionSpec as P

HEAD_DIM = 64
SIDE = 4
PIECES = 4
SLOTS = 2
epsilon = 1e-06
MESH = pl.DeviceIdType.MESH
f32 = jnp.float32
bf16 = jnp.bfloat16


def attend_kernel(
    n_dp,
    n_tp,
    retrieved_ref,
    location_ref,
    questions_ref,
    memory_ref,
    gain_ref,
    wq_hbm,
    wk_hbm,
    wv_hbm,
    context_ref,
    table,
    tables,
    tables_s,
    place_s,
    outbox,
    inbox0,
    inbox1,
    inbox2,
    inbox3,
    gathered,
    asked,
    wq,
    wkv,
    total,
    squares,
    asked_total,
    asked_squares,
    keys,
    values,
    w_sem,
    tables_sem,
    table_send,
    table_recv,
    asked_send,
    asked_recv,
    fetch_send,
    fetch_recv,
    ring_send,
    ring_recv,
):
    inboxes = (inbox0, inbox1, inbox2, inbox3)
    held, tokens, width = memory_ref.shape
    question_tokens = questions_ref.shape[0]
    requests = retrieved_ref.shape[1]
    piece = tokens // PIECES
    rows = requests * piece
    half = rows // 2
    quarter = rows // 4
    full_width = n_tp * width
    heads = width // HEAD_DIM
    d = lax.axis_index("dp")
    t = lax.axis_index("tensor")
    x, y = lax.rem(t, SIDE), lax.div(t, SIDE)

    def at(dx, dy):
        return lax.rem(y + dy + SIDE, SIDE) * SIDE + lax.rem(x + dx + SIDE, SIDE)

    w_copies = [
        pltpu.make_async_copy(wq_hbm, wq, w_sem.at[0]),
        pltpu.make_async_copy(wk_hbm, wkv.at[:, :, pl.ds(0, width)], w_sem.at[1]),
        pltpu.make_async_copy(wv_hbm, wkv.at[:, :, pl.ds(width, width)], w_sem.at[2]),
    ]
    for copy in w_copies:
        copy.start()

    barrier = pltpu.get_barrier_semaphore()

    @pl.loop(1, n_dp)
    def _(k):
        pl.semaphore_signal(barrier, inc=1, device_id={"dp": lax.rem(d + k, n_dp)}, device_id_type=MESH)

    @pl.loop(1, n_tp)
    def _(k):
        pl.semaphore_signal(barrier, inc=1, device_id={"tensor": lax.rem(t + k, n_tp)}, device_id_type=MESH)

    stored = [location_ref[retrieved_ref[0, j]] for j in range(requests)]
    owners = [s // held for s in stored]
    local = [s % held for s in stored]
    lane = lax.broadcasted_iota(jnp.int32, (8, 128), 1)
    first = jnp.zeros((8, 128), jnp.int32)
    last = jnp.zeros((8, 128), jnp.int32)
    for j in range(requests):
        last = jnp.where(lane == owners[j], local[j], last)
    for j in reversed(range(requests)):
        first = jnp.where(lane == owners[j], local[j], first)
    sub = lax.broadcasted_iota(jnp.int32, (8, 128), 0)
    table[...] = jnp.where(sub == 0, first, last)
    for j in range(requests):
        again = jnp.int32(0)
        for i in range(j):
            again = jnp.where(owners[i] == owners[j], jnp.int32(1), again)
        place_s[j] = owners[j] * SLOTS + again

    tables[pl.ds(d, 1)] = table[...][None]
    asked[pl.ds(t, 1)] = questions_ref[...][None]

    pl.semaphore_wait(barrier, n_dp + n_tp - 2)

    def table_copy(k):
        return pltpu.make_async_remote_copy(
            src_ref=table,
            dst_ref=tables.at[d],
            send_sem=table_send.at[k],
            recv_sem=table_recv.at[k],
            device_id={"dp": lax.rem(d + k, n_dp)},
            device_id_type=MESH,
        )

    def asked_copy(k):
        return pltpu.make_async_remote_copy(
            src_ref=questions_ref,
            dst_ref=asked.at[t],
            send_sem=asked_send.at[k],
            recv_sem=asked_recv.at[k],
            device_id={"tensor": lax.rem(t + k, n_tp)},
            device_id_type=MESH,
        )

    def table_arrival(k):
        return pltpu.make_async_remote_copy(
            src_ref=table,
            dst_ref=tables.at[lax.rem(d + n_dp - k, n_dp)],
            send_sem=table_send.at[k],
            recv_sem=table_recv.at[k],
            device_id={"dp": lax.rem(d + k, n_dp)},
            device_id_type=MESH,
        )

    def asked_arrival(k):
        return pltpu.make_async_remote_copy(
            src_ref=questions_ref,
            dst_ref=asked.at[lax.rem(t + n_tp - k, n_tp)],
            send_sem=asked_send.at[k],
            recv_sem=asked_recv.at[k],
            device_id={"tensor": lax.rem(t + k, n_tp)},
            device_id_type=MESH,
        )

    @pl.loop(1, n_dp)
    def _(k):
        table_copy(k).start()

    @pl.loop(1, n_tp)
    def _(k):
        asked_copy(k).start()

    @pl.loop(1, n_dp)
    def _(k):
        table_arrival(k).wait_recv()

    to_scalar = pltpu.make_async_copy(tables, tables_s, tables_sem)
    to_scalar.start()
    to_scalar.wait()

    def fetch_copy(c, k, sender):
        return pltpu.make_async_remote_copy(
            src_ref=outbox.at[c, k],
            dst_ref=inboxes[c].at[pl.ds(sender * SLOTS, SLOTS)],
            send_sem=fetch_send.at[c, k],
            recv_sem=fetch_recv.at[c, k],
            device_id={"dp": lax.rem(d + k, n_dp)},
            device_id_type=MESH,
        )

    for c in range(PIECES):
        span = pl.ds(c * piece, piece)

        @pl.loop(1, n_dp)
        def _(k):
            asker = lax.rem(d + k, n_dp)
            for s in range(SLOTS):
                outbox[c, k, s] = memory_ref[tables_s[asker, s, d], span, :]
            fetch_copy(c, k, d).start()

        for s in range(SLOTS):
            inboxes[c][pl.ds(d * SLOTS + s, 1)] = memory_ref[tables_s[d, s, d], span, :][None]

    for copy in w_copies:
        copy.wait()

    @pl.loop(1, n_tp)
    def _(k):
        asked_arrival(k).wait_recv()

    asked_total[...] = jnp.zeros_like(asked_total)
    asked_squares[...] = jnp.zeros_like(asked_squares)

    @pl.loop(0, n_tp)
    def _(s):
        wide = asked[s].astype(f32)
        normed = (wide * gain_ref[pl.ds(s, 1), :]).astype(bf16)
        asked_squares[...] += jnp.sum(wide * wide, axis=1, keepdims=True)
        asked_total[:, :width] += jnp.dot(normed, wq[s], preferred_element_type=f32)
        asked_total[:, width:] += jnp.dot(normed, wkv[s], preferred_element_type=f32)

    asked_scale = lax.rsqrt(asked_squares[:, :1] / full_width + epsilon)
    projected = (asked_total[...] * asked_scale).astype(bf16)
    own_query = projected[:, :width] * jnp.asarray(HEAD_DIM ** (-0.5), bf16)
    own_key = projected[:, width : 2 * width]
    own_value = projected[:, 2 * width :]
    head_of = lax.broadcasted_iota(jnp.int32, (question_tokens, width), 1) // HEAD_DIM
    spread = jnp.concatenate(
        [jnp.where(head_of == h, own_query, jnp.zeros_like(own_query)) for h in range(heads)], axis=0
    )

    def dot_t(a, b):
        return lax.dot_general(a, b, (((1,), (1,)), ((), ())), preferred_element_type=f32)

    own_scores = dot_t(spread, own_key)
    own_most = jnp.max(own_scores, axis=1, keepdims=True)

    def ring(c, kind, h, direction, k, arrival):
        sign = 1 if direction == 0 else -1
        mine = 0 if not arrival else -sign
        if kind in ("own", "pass"):
            step = (sign, 0) if h == 0 else (0, sign)
            back = (mine, 0) if h == 0 else (0, mine)
            if kind == "own":
                origin = at(*back)
            else:
                origin = at(*(tuple(b - s for b, s in zip(back, step))))
            index = {"own": 0, "pass": 2}[kind] + direction
        else:
            step = (0, sign) if h == 0 else (sign, 0)
            back = (0, mine) if h == 0 else (mine, 0)
            if kind == "turnpass":
                back = tuple(b - s for b, s in zip(back, step))
            shift = (k, 0) if h == 0 else (0, k)
            origin = at(*(b + s for b, s in zip(back, shift)))
            index = {"turn": 4, "turnpass": 12}[kind] + direction * 4 + k % 4
        if kind in ("pass", "turnpass"):
            span = pl.ds(h * half + direction * quarter, quarter)
        else:
            span = pl.ds(h * half, half)
        place = gathered.at[c, origin, span]
        return pltpu.make_async_remote_copy(
            src_ref=place,
            dst_ref=place,
            send_sem=ring_send.at[c, h * 20 + index],
            recv_sem=ring_recv.at[c, h * 20 + index],
            device_id={"tensor": at(*step)},
            device_id_type=MESH,
        )

    def begin(c):
        @pl.loop(1, n_dp)
        def _(k):
            fetch_copy(c, k, lax.rem(d + n_dp - k, n_dp)).wait_recv()

        for j in range(requests):
            gathered[c, pl.ds(t, 1), j * piece : (j + 1) * piece] = inboxes[c][place_s[j]][None]
        for h in range(2):
            for direction in range(2):
                ring(c, "own", h, direction, 0, False).start()
        for h in range(2):
            for direction in range(2):
                ring(c, "turn", h, direction, 0, False).start()

    def middle(c):
        for direction in range(2):
            k = -1 if direction == 0 else 1
            for h in range(2):
                ring(c, "own", h, direction, 0, True).wait_recv()
                ring(c, "pass", h, direction, 0, False).start()
                for turned in range(2):
                    ring(c, "turn", h, turned, k, False).start()
        for h in range(2):
            for direction in range(2):
                ring(c, "pass", h, direction, 0, True).wait_recv()
            for turned in range(2):
                ring(c, "turn", h, turned, 2, False).start()

    def turn_arrivals(c, k):
        for direction in range(2):
            for h in range(2):
                ring(c, "turn", h, direction, k, True).wait_recv()
                ring(c, "turnpass", h, direction, k, False).start()

    def last_arrivals(c):
        for k in (0, -1, 1, 2):
            for direction in range(2):
                for h in range(2):
                    ring(c, "turnpass", h, direction, k, True).wait_recv()

    def multiply(c, low, high):
        @pl.loop(low, high)
        def _(s):
            wide = gathered[c, s].astype(f32)
            normed = (wide * gain_ref[pl.ds(s, 1), :]).astype(bf16)
            squared = wide * wide
            folded = squared[:, :128]
            for part in range(1, width // 128):
                folded = folded + squared[:, part * 128 : (part + 1) * 128]
            squares[...] += folded
            total[...] += jnp.dot(normed, wkv[s], preferred_element_type=f32)

    def clear():
        total[...] = jnp.zeros_like(total)
        squares[...] = jnp.zeros_like(squares)

    def finish(c):
        scale = lax.rsqrt(jnp.sum(squares[...], axis=1, keepdims=True) / full_width + epsilon)
        span = pl.ds(c * piece, piece)
        key = (total[:, :width] * scale).astype(bf16)
        keys[:, span, :] = key.reshape(requests, piece, width)
        value = (total[:, width:] * scale).astype(bf16)
        values[:, span, :] = value.reshape(requests, piece, width)

    quarter_tp = n_tp // 4
    begin(0)
    for c in range(PIECES):
        middle(c)
        if c > 0:
            last_arrivals(c - 1)
            clear()
            multiply(c - 1, 0, quarter_tp)
        if c + 1 < PIECES:
            begin(c + 1)
        for i, k in enumerate((0, -1, 1, 2)):
            turn_arrivals(c, k)
            if c > 0 and i < 3:
                multiply(c - 1, (i + 1) * quarter_tp, (i + 2) * quarter_tp)
        if c > 0:
            finish(c - 1)
    last_arrivals(PIECES - 1)
    clear()
    multiply(PIECES - 1, 0, n_tp)
    finish(PIECES - 1)

    @pl.loop(0, requests)
    def _(j):
        scores = dot_t(spread, keys[j])
        most = jnp.maximum(own_most, jnp.max(scores, axis=1, keepdims=True))
        far = jnp.exp(scores - most)
        own = jnp.exp(own_scores - most)
        mass = jnp.sum(far, axis=1, keepdims=True) + jnp.sum(own, axis=1, keepdims=True)
        out = jnp.dot((far / mass).astype(bf16), values[j], preferred_element_type=f32)
        out += jnp.dot((own / mass).astype(bf16), own_value, preferred_element_type=f32)
        context = jnp.zeros((question_tokens, width), f32)
        for h in range(heads):
            block = out[h * question_tokens : (h + 1) * question_tokens]
            context = context + jnp.where(head_of == h, block, jnp.zeros_like(block))
        context_ref[j] = context.astype(bf16)

    @pl.loop(1, n_dp)
    def _(k):
        table_copy(k).wait_send()
        for c in range(PIECES):
            fetch_copy(c, k, d).wait_send()

    @pl.loop(1, n_tp)
    def _(k):
        asked_copy(k).wait_send()

    @pl.loop(0, PIECES)
    def _(c):
        for h in range(2):
            for direction in range(2):
                for kind in ("own", "pass"):
                    ring(c, kind, h, direction, 0, False).wait_send()
                for k in range(4):
                    for kind in ("turn", "turnpass"):
                        ring(c, kind, h, direction, k, False).wait_send()


def on_device(questions, memory, retrieved, location, norm_gain, w_query, w_key, w_value, w_out):
    n_dp, n_tp = lax.axis_size("dp"), lax.axis_size("tensor")
    question_count, question_tokens, width = questions.shape
    held, tokens, _ = memory.shape
    requests = retrieved.shape[1]
    heads_width = w_key.shape[1]
    piece = tokens // PIECES
    rows = requests * piece
    sem = pltpu.SemaphoreType.DMA
    vmem = pl.BlockSpec(memory_space=pltpu.VMEM)
    smem = pl.BlockSpec(memory_space=pltpu.SMEM)
    hbm = pl.BlockSpec(memory_space=pl.ANY)
    context = pl.pallas_call(
        functools.partial(attend_kernel, n_dp, n_tp),
        out_shape=jax.ShapeDtypeStruct((requests, question_tokens, heads_width), bf16),
        in_specs=[smem, smem, vmem, vmem, vmem, hbm, hbm, hbm],
        out_specs=vmem,
        scratch_shapes=[
            pltpu.VMEM((8, 128), jnp.int32),
            pltpu.VMEM((n_dp, 8, 128), jnp.int32),
            pltpu.SMEM((n_dp, 8, 128), jnp.int32),
            pltpu.SMEM((requests,), jnp.int32),
            pltpu.VMEM((PIECES, n_dp, SLOTS, piece, width), bf16),
            pltpu.VMEM((n_dp * SLOTS, piece, width), bf16),
            pltpu.VMEM((n_dp * SLOTS, piece, width), bf16),
            pltpu.VMEM((n_dp * SLOTS, piece, width), bf16),
            pltpu.VMEM((n_dp * SLOTS, piece, width), bf16),
            pltpu.VMEM((PIECES, n_tp, rows, width), bf16),
            pltpu.VMEM((n_tp, question_tokens, width), bf16),
            pltpu.VMEM((n_tp, width, heads_width), bf16),
            pltpu.VMEM((n_tp, width, 2 * heads_width), bf16),
            pltpu.VMEM((rows, 2 * heads_width), f32),
            pltpu.VMEM((rows, 128), f32),
            pltpu.VMEM((question_tokens, 3 * heads_width), f32),
            pltpu.VMEM((question_tokens, 128), f32),
            pltpu.VMEM((requests, tokens, heads_width), bf16),
            pltpu.VMEM((requests, tokens, heads_width), bf16),
            sem((3,)),
            sem,
            sem((n_dp,)),
            sem((n_dp,)),
            sem((n_tp,)),
            sem((n_tp,)),
            sem((PIECES, n_dp)),
            sem((PIECES, n_dp)),
            sem((PIECES, 40)),
            sem((PIECES, 40)),
        ],
        compiler_params=pltpu.CompilerParams(
            collective_id=0, has_side_effects=True, vmem_limit_bytes=56 * 1024 * 1024
        ),
        name="fetch_gather_attend",
    )(
        retrieved,
        location,
        questions.reshape(question_tokens, width),
        memory,
        norm_gain.reshape(n_tp, width),
        w_query.reshape(n_tp, width, heads_width),
        w_key.reshape(n_tp, width, heads_width),
        w_value.reshape(n_tp, width, heads_width),
    )
    context = context.reshape(requests * question_tokens, heads_width)
    head_term = jnp.dot(context, w_out, preferred_element_type=f32).astype(bf16)
    summed = lax.psum_scatter(head_term, "tensor", scatter_dimension=1, tiled=True).astype(f32)
    summed = summed.reshape(question_count, requests, question_tokens, width)
    return (questions.astype(f32)[:, None] + summed).astype(bf16)


def solution(mesh):
    placed = (
        P("dp", None, "tensor"),
        P("dp", None, "tensor"),
        P("dp", None),
        P(),
        P(),
        P(None, "tensor"),
        P(None, "tensor"),
        P(None, "tensor"),
        P("tensor", None),
    )
    return jax.shard_map(
        on_device,
        mesh=mesh,
        in_specs=placed,
        out_specs=P("dp", None, None, "tensor"),
        check_vma=False,
    )
```

```python
import functools

import jax
import jax.numpy as jnp
from jax import lax
from jax.experimental import pallas as pl
from jax.experimental.pallas import tpu as pltpu
from jax.sharding import PartitionSpec as P

HEAD_DIM = 64
SIDE = 4
PIECES = 4
SLOTS = 2
epsilon = 1e-06
MESH = pl.DeviceIdType.MESH
f32 = jnp.float32
bf16 = jnp.bfloat16


def attend_kernel(
    n_dp,
    n_tp,
    retrieved_ref,
    location_ref,
    questions_hbm,
    memory_hbm,
    gain_hbm,
    wq_hbm,
    wk_hbm,
    wv_hbm,
    wo_hbm,
    updated_ref,
    questions_ref,
    memory_ref,
    gain_ref,
    table,
    tables,
    tables_s,
    place_s,
    outbox,
    inbox0,
    inbox1,
    inbox2,
    inbox3,
    gathered,
    asked,
    wq,
    wkv,
    wo,
    contexts,
    far_out,
    far_in,
    near_out,
    near_in,
    line_sum,
    last_far_out,
    last_far_in,
    last_near_out,
    last_near_in,
    total,
    squares,
    asked_total,
    asked_squares,
    keys,
    values,
    w_sem,
    in_sem,
    tables_sem,
    table_send,
    table_recv,
    asked_send,
    asked_recv,
    fetch_send,
    fetch_recv,
    ring_send,
    ring_recv,
    sum_send,
    sum_recv,
):
    inboxes = (inbox0, inbox1, inbox2, inbox3)
    held, tokens, width = memory_ref.shape
    question_tokens = questions_ref.shape[0]
    requests = retrieved_ref.shape[1]
    piece = tokens // PIECES
    rows = requests * piece
    half = rows // 2
    quarter = rows // 4
    full_width = n_tp * width
    heads = width // HEAD_DIM
    d = lax.axis_index("dp")
    t = lax.axis_index("tensor")
    x, y = lax.rem(t, SIDE), lax.div(t, SIDE)

    def gain(s):
        return gain_ref[:, pl.ds(pl.multiple_of(s * width, 128), width)]

    def at(dx, dy):
        return lax.rem(y + dy + SIDE, SIDE) * SIDE + lax.rem(x + dx + SIDE, SIDE)

    in_copies = [
        pltpu.make_async_copy(memory_hbm, memory_ref, in_sem.at[0]),
        pltpu.make_async_copy(questions_hbm, questions_ref, in_sem.at[1]),
        pltpu.make_async_copy(gain_hbm, gain_ref, in_sem.at[2]),
    ]
    for copy in in_copies:
        copy.start()

    w_copies = [
        pltpu.make_async_copy(wq_hbm, wq, w_sem.at[0]),
        pltpu.make_async_copy(wk_hbm, wkv.at[:, :, pl.ds(0, width)], w_sem.at[1]),
        pltpu.make_async_copy(wv_hbm, wkv.at[:, :, pl.ds(width, width)], w_sem.at[2]),
        pltpu.make_async_copy(wo_hbm, wo, w_sem.at[3]),
    ]
    for copy in w_copies:
        copy.start()

    barrier = pltpu.get_barrier_semaphore()

    @pl.loop(1, n_dp)
    def _(k):
        pl.semaphore_signal(barrier, inc=1, device_id={"dp": lax.rem(d + k, n_dp)}, device_id_type=MESH)

    for k in range(1, SIDE):
        pl.semaphore_signal(barrier, inc=1, device_id={"tensor": at(k, 0)}, device_id_type=MESH)
        pl.semaphore_signal(barrier, inc=1, device_id={"tensor": at(0, k)}, device_id_type=MESH)

    stored = [location_ref[retrieved_ref[0, j]] for j in range(requests)]
    owners = [s // held for s in stored]
    local = [s % held for s in stored]
    lane = lax.broadcasted_iota(jnp.int32, (8, 128), 1)
    first = jnp.zeros((8, 128), jnp.int32)
    last = jnp.zeros((8, 128), jnp.int32)
    for j in range(requests):
        last = jnp.where(lane == owners[j], local[j], last)
    for j in reversed(range(requests)):
        first = jnp.where(lane == owners[j], local[j], first)
    sub = lax.broadcasted_iota(jnp.int32, (8, 128), 0)
    table[...] = jnp.where(sub == 0, first, last)
    for j in range(requests):
        again = jnp.int32(0)
        for i in range(j):
            again = jnp.where(owners[i] == owners[j], jnp.int32(1), again)
        place_s[j] = owners[j] * SLOTS + again

    tables[pl.ds(d, 1)] = table[...][None]
    in_copies[1].wait()
    asked[pl.ds(t, 1)] = questions_ref[...][None]

    pl.semaphore_wait(barrier, n_dp - 1 + 2 * (SIDE - 1))

    def table_copy(k):
        return pltpu.make_async_remote_copy(
            src_ref=table,
            dst_ref=tables.at[d],
            send_sem=table_send.at[k],
            recv_sem=table_recv.at[k],
            device_id={"dp": lax.rem(d + k, n_dp)},
            device_id_type=MESH,
        )

    def asked_copy(level, k, back):
        if level == 0:
            place = asked.at[at(-back, 0)]
            target = at(k, 0)
        else:
            place = asked.at[pl.ds(lax.rem(y - back + SIDE, SIDE) * SIDE, SIDE)]
            target = at(0, k)
        return pltpu.make_async_remote_copy(
            src_ref=place,
            dst_ref=place,
            send_sem=asked_send.at[level * 3 + k - 1],
            recv_sem=asked_recv.at[level * 3 + k - 1],
            device_id={"tensor": target},
            device_id_type=MESH,
        )

    def table_arrival(k):
        return pltpu.make_async_remote_copy(
            src_ref=table,
            dst_ref=tables.at[lax.rem(d + n_dp - k, n_dp)],
            send_sem=table_send.at[k],
            recv_sem=table_recv.at[k],
            device_id={"dp": lax.rem(d + k, n_dp)},
            device_id_type=MESH,
        )

    @pl.loop(1, n_dp)
    def _(k):
        table_copy(k).start()

    for k in range(1, SIDE):
        asked_copy(0, k, 0).start()
    in_copies[0].wait()

    @pl.loop(1, n_dp)
    def _(k):
        table_arrival(k).wait_recv()

    to_scalar = pltpu.make_async_copy(tables, tables_s, tables_sem)
    to_scalar.start()
    to_scalar.wait()

    def fetch_copy(c, k, sender):
        return pltpu.make_async_remote_copy(
            src_ref=outbox.at[c, k],
            dst_ref=inboxes[c].at[pl.ds(sender * SLOTS, SLOTS)],
            send_sem=fetch_send.at[c, k],
            recv_sem=fetch_recv.at[c, k],
            device_id={"dp": lax.rem(d + k, n_dp)},
            device_id_type=MESH,
        )

    for c in range(PIECES):
        span = pl.ds(c * piece, piece)

        @pl.loop(1, n_dp)
        def _(k):
            asker = lax.rem(d + k, n_dp)
            for s in range(SLOTS):
                outbox[c, k, s] = memory_ref[tables_s[asker, s, d], span, :]
            fetch_copy(c, k, d).start()

        for s in range(SLOTS):
            inboxes[c][pl.ds(d * SLOTS + s, 1)] = memory_ref[tables_s[d, s, d], span, :][None]

    for k in range(1, SIDE):
        asked_copy(0, k, k).wait_recv()
    for k in range(1, SIDE):
        asked_copy(1, k, 0).start()

    def ring(c, kind, h, direction, k, arrival):
        sign = 1 if direction == 0 else -1
        mine = 0 if not arrival else -sign
        if kind in ("own", "pass"):
            step = (sign, 0) if h == 0 else (0, sign)
            back = (mine, 0) if h == 0 else (0, mine)
            if kind == "own":
                origin = at(*back)
            else:
                origin = at(*(tuple(b - s for b, s in zip(back, step))))
            index = {"own": 0, "pass": 2}[kind] + direction
        else:
            step = (0, sign) if h == 0 else (sign, 0)
            back = (0, mine) if h == 0 else (mine, 0)
            if kind == "turnpass":
                back = tuple(b - s for b, s in zip(back, step))
            shift = (k, 0) if h == 0 else (0, k)
            origin = at(*(b + s for b, s in zip(back, shift)))
            index = {"turn": 4, "turnpass": 12}[kind] + direction * 4 + k % 4
        if kind in ("pass", "turnpass"):
            span = pl.ds(h * half + direction * quarter, quarter)
        else:
            span = pl.ds(h * half, half)
        place = gathered.at[c, origin, span]
        return pltpu.make_async_remote_copy(
            src_ref=place,
            dst_ref=place,
            send_sem=ring_send.at[c, h * 20 + index],
            recv_sem=ring_recv.at[c, h * 20 + index],
            device_id={"tensor": at(*step)},
            device_id_type=MESH,
        )

    def begin(c):
        @pl.loop(1, n_dp)
        def _(k):
            fetch_copy(c, k, lax.rem(d + n_dp - k, n_dp)).wait_recv()

        for j in range(requests):
            gathered[c, pl.ds(t, 1), j * piece : (j + 1) * piece] = inboxes[c][place_s[j]][None]
        for h in range(2):
            for direction in range(2):
                ring(c, "own", h, direction, 0, False).start()

    def along(c):
        for direction in range(2):
            for h in range(2):
                ring(c, "own", h, direction, 0, True).wait_recv()
                ring(c, "pass", h, direction, 0, False).start()

    def turn(c, k):
        for h in range(2):
            if k == 2:
                for direction in range(2):
                    ring(c, "pass", h, direction, 0, True).wait_recv()
            for direction in range(2):
                ring(c, "turn", h, direction, k, False).start()

    def turn_arrivals(c, k):
        for direction in range(2):
            for h in range(2):
                ring(c, "turn", h, direction, k, True).wait_recv()
                ring(c, "turnpass", h, direction, k, False).start()

    def last_arrivals(c):
        for k in (0, -1, 1, 2):
            for direction in range(2):
                for h in range(2):
                    ring(c, "turnpass", h, direction, k, True).wait_recv()

    def multiply(c, s):
        wide = gathered[c, s].astype(f32)
        normed = (wide * gain(s)).astype(bf16)
        squared = wide * wide
        folded = squared[:, :128]
        for part in range(1, width // 128):
            folded = folded + squared[:, part * 128 : (part + 1) * 128]
        squares[...] += folded
        total[...] += jnp.dot(normed, wkv[s], preferred_element_type=f32)

    def multiply_range(c, low, high):
        @pl.loop(low, high)
        def _(s):
            multiply(c, s)

    def clear():
        total[...] = jnp.zeros_like(total)
        squares[...] = jnp.zeros_like(squares)

    def finish(c):
        scale = lax.rsqrt(jnp.sum(squares[...], axis=1, keepdims=True) / full_width + epsilon)
        span = pl.ds(c * piece, piece)
        key = (total[:, :width] * scale).astype(bf16)
        keys[:, span, :] = key.reshape(requests, piece, width)
        value = (total[:, width:] * scale).astype(bf16)
        values[:, span, :] = value.reshape(requests, piece, width)

    def ask():
        for copy in w_copies:
            copy.wait()

        in_copies[2].wait()
        for k in range(1, SIDE):
            asked_copy(1, k, k).wait_recv()

        asked_total[...] = jnp.zeros_like(asked_total)
        asked_squares[...] = jnp.zeros_like(asked_squares)

        @pl.loop(0, n_tp)
        def _(s):
            wide = asked[s].astype(f32)
            normed = (wide * gain(s)).astype(bf16)
            asked_squares[...] += jnp.sum(wide * wide, axis=1, keepdims=True)
            asked_total[:, :width] += jnp.dot(normed, wq[s], preferred_element_type=f32)
            asked_total[:, width:] += jnp.dot(normed, wkv[s], preferred_element_type=f32)

    quarter_tp = n_tp // 4
    last_piece = PIECES - 1
    begin(0)
    for c in range(PIECES):
        along(c)
        for k in (0, -1, 1):
            turn(c, k)
        if c == 0:
            ask()
        if c < last_piece:
            begin(c + 1)
        turn(c, 2)
        if c > 1:
            last_arrivals(c - 2)
            clear()
        for i, k in enumerate((0, -1, 1, 2)):
            if c > 0:
                turn_arrivals(c - 1, k)
            if c > 1:
                multiply_range(c - 2, i * quarter_tp, (i + 1) * quarter_tp)
        if c > 1:
            finish(c - 2)
    last_arrivals(last_piece - 1)
    clear()
    for i, k in enumerate((0, -1, 1, 2)):
        turn_arrivals(last_piece, k)
        multiply_range(last_piece - 1, i * quarter_tp, (i + 1) * quarter_tp)
    finish(last_piece - 1)
    clear()

    @pl.loop(0, 9)
    def _(i):
        multiply(last_piece, at(lax.rem(i, 3) - 1, lax.div(i, 3) - 1))

    last_arrivals(last_piece)

    @pl.loop(0, 7)
    def _(i):
        multiply(last_piece, at(lax.select(i < 4, 2, i - 5), lax.select(i < 4, i - 1, 2)))

    finish(last_piece)

    asked_scale = lax.rsqrt(asked_squares[:, :1] / full_width + epsilon)
    projected = (asked_total[...] * asked_scale).astype(bf16)
    own_query = projected[:, :width] * jnp.asarray(HEAD_DIM ** (-0.5), bf16)
    own_key = projected[:, width : 2 * width]
    own_value = projected[:, 2 * width :]
    head_of = lax.broadcasted_iota(jnp.int32, (question_tokens, width), 1) // HEAD_DIM
    spread = jnp.concatenate(
        [jnp.where(head_of == h, own_query, jnp.zeros_like(own_query)) for h in range(heads)], axis=0
    )

    def dot_t(a, b):
        return lax.dot_general(a, b, (((1,), (1,)), ((), ())), preferred_element_type=f32)

    own_scores = dot_t(spread, own_key)
    own_most = jnp.max(own_scores, axis=1, keepdims=True)

    def attend(j):
        scores = dot_t(spread, keys[j])
        most = jnp.maximum(own_most, jnp.max(scores, axis=1, keepdims=True))
        far = jnp.exp(scores - most)
        own = jnp.exp(own_scores - most)
        mass = jnp.sum(far, axis=1, keepdims=True) + jnp.sum(own, axis=1, keepdims=True)
        share = 1.0 / mass
        out = jnp.dot((far * share).astype(bf16), values[j], preferred_element_type=f32)
        out += jnp.dot((own * share).astype(bf16), own_value, preferred_element_type=f32)
        context = jnp.zeros((question_tokens, width), f32)
        for h in range(heads):
            block = out[h * question_tokens : (h + 1) * question_tokens]
            context = context + jnp.where(head_of == h, block, jnp.zeros_like(block))
        contexts[j] = context.astype(bf16)

    part = requests // 2
    part_rows = part * question_tokens
    part_half = part_rows // 2

    def aim(h, k1, k2):
        return at(k1, k2) if h == 0 else at(k2, k1)

    def term(h, low, count, s):
        rows_in = contexts[h * part : (h + 1) * part].reshape(part_rows, width)[low : low + count]
        columns = wo[:, pl.ds(pl.multiple_of(s * width, 128), width)]
        return jnp.dot(rows_in, columns, preferred_element_type=f32)

    def hop(kind, h, direction, k):
        sign = 1 if direction == 0 else -1
        k = k % 4
        if kind == "far":
            src, dst, index = far_out.at[h, direction, k], far_in.at[h, direction, k], direction * 4 + k
        elif kind == "near":
            src, dst, index = near_out.at[h, direction, k], near_in.at[h, direction, k], 8 + direction * 4 + k
        elif kind == "last_far":
            src, dst, index = last_far_out.at[h, direction], last_far_in.at[h, direction], 16 + direction
        else:
            src, dst, index = last_near_out.at[h, direction], last_near_in.at[h, direction], 18 + direction
        target = aim(h, sign, 0) if kind in ("far", "near") else aim(h, 0, sign)
        return pltpu.make_async_remote_copy(
            src_ref=src,
            dst_ref=dst,
            send_sem=sum_send.at[h * 20 + index],
            recv_sem=sum_recv.at[h * 20 + index],
            device_id={"tensor": target},
            device_id_type=MESH,
        )

    order = (2, 1, -1, 0)

    def send_far(h):
        for k in order:
            for direction in range(2):
                far_out[h, direction, k % 4] = term(h, direction * part_half, part_half, aim(h, 2, k)).astype(bf16)
                hop("far", h, direction, k).start()

    def send_near(h, k):
        for direction in range(2):
            sign = 1 if direction == 0 else -1
            low = direction * part_half
            here = term(h, 0, part_rows, aim(h, sign, k))
            hop("far", h, direction, k).wait_recv()
            passed = here[low : low + part_half] + far_in[h, direction, k % 4].astype(f32)
            other = part_half - low
            near_out[h, direction, k % 4, low : low + part_half] = passed.astype(bf16)
            near_out[h, direction, k % 4, other : other + part_half] = here[other : other + part_half].astype(bf16)
            hop("near", h, direction, k).start()

    def sum_line(h, k):
        here = term(h, 0, part_rows, aim(h, 0, k))
        for direction in range(2):
            hop("near", h, direction, k).wait_recv()
            here = here + near_in[h, direction, k % 4].astype(f32)
        line_sum[h, k % 4] = here

    def send_last_far(h):
        for direction in range(2):
            low = direction * part_half
            last_far_out[h, direction] = line_sum[h, 2, low : low + part_half].astype(bf16)
            hop("last_far", h, direction, 0).start()

    def send_last_near(h):
        for direction in range(2):
            k = 1 if direction == 0 else 3
            low = direction * part_half
            other = part_half - low
            hop("last_far", h, direction, 0).wait_recv()
            passed = line_sum[h, k, low : low + part_half] + last_far_in[h, direction].astype(f32)
            last_near_out[h, direction, low : low + part_half] = passed.astype(bf16)
            last_near_out[h, direction, other : other + part_half] = line_sum[h, k, other : other + part_half].astype(bf16)
            hop("last_near", h, direction, 0).start()

    def settle(h):
        summed = line_sum[h, 0]
        for direction in range(2):
            hop("last_near", h, direction, 0).wait_recv()
            summed = summed + last_near_in[h, direction].astype(f32)
        summed = summed.reshape(part, question_tokens, width)
        updated_ref[h * part : (h + 1) * part] = (questions_ref[...].astype(f32)[None] + summed).astype(bf16)

    for h in range(2):

        for j in range(h * part, (h + 1) * part):
            attend(j)

        send_far(h)
    for k in order:
        for h in range(2):
            send_near(h, k)
    for k in order:
        for h in range(2):
            sum_line(h, k)
            if k == 2:
                send_last_far(h)
            if k == -1:
                send_last_near(h)
    for h in range(2):
        settle(h)

    @pl.loop(1, n_dp)
    def _(k):
        table_copy(k).wait_send()
        for c in range(PIECES):
            fetch_copy(c, k, d).wait_send()

    for level in range(2):
        for k in range(1, SIDE):
            asked_copy(level, k, 0).wait_send()

    @pl.loop(0, PIECES)
    def _(c):
        for h in range(2):
            for direction in range(2):
                for kind in ("own", "pass"):
                    ring(c, kind, h, direction, 0, False).wait_send()
                for k in range(4):
                    for kind in ("turn", "turnpass"):
                        ring(c, kind, h, direction, k, False).wait_send()

    for h in range(2):
        for direction in range(2):
            for k in range(4):
                for kind in ("far", "near"):
                    hop(kind, h, direction, k).wait_send()
            for kind in ("last_far", "last_near"):
                hop(kind, h, direction, 0).wait_send()


def on_device(questions, memory, retrieved, location, norm_gain, w_query, w_key, w_value, w_out):
    n_dp, n_tp = lax.axis_size("dp"), lax.axis_size("tensor")
    question_count, question_tokens, width = questions.shape
    held, tokens, _ = memory.shape
    requests = retrieved.shape[1]
    heads_width = w_key.shape[1]
    piece = tokens // PIECES
    rows = requests * piece
    part_rows = (requests // 2) * question_tokens
    part_half = part_rows // 2
    sem = pltpu.SemaphoreType.DMA
    vmem = pl.BlockSpec(memory_space=pltpu.VMEM)
    smem = pl.BlockSpec(memory_space=pltpu.SMEM)
    hbm = pl.BlockSpec(memory_space=pl.ANY)
    updated = pl.pallas_call(
        functools.partial(attend_kernel, n_dp, n_tp),
        out_shape=jax.ShapeDtypeStruct((requests, question_tokens, width), bf16),
        in_specs=[smem, smem] + [hbm] * 7,
        out_specs=vmem,
        scratch_shapes=[
            pltpu.VMEM((question_tokens, width), bf16),
            pltpu.VMEM((held, tokens, width), bf16),
            pltpu.VMEM((1, n_tp * width), f32),
            pltpu.VMEM((8, 128), jnp.int32),
            pltpu.VMEM((n_dp, 8, 128), jnp.int32),
            pltpu.SMEM((n_dp, 8, 128), jnp.int32),
            pltpu.SMEM((requests,), jnp.int32),
            pltpu.VMEM((PIECES, n_dp, SLOTS, piece, width), bf16),
            pltpu.VMEM((n_dp * SLOTS, piece, width), bf16),
            pltpu.VMEM((n_dp * SLOTS, piece, width), bf16),
            pltpu.VMEM((n_dp * SLOTS, piece, width), bf16),
            pltpu.VMEM((n_dp * SLOTS, piece, width), bf16),
            pltpu.VMEM((PIECES, n_tp, rows, width), bf16),
            pltpu.VMEM((n_tp, question_tokens, width), bf16),
            pltpu.VMEM((n_tp, width, heads_width), bf16),
            pltpu.VMEM((n_tp, width, 2 * heads_width), bf16),
            pltpu.VMEM((heads_width, n_tp * width), bf16),
            pltpu.VMEM((requests, question_tokens, heads_width), bf16),
            pltpu.VMEM((2, 2, SIDE, part_half, width), bf16),
            pltpu.VMEM((2, 2, SIDE, part_half, width), bf16),
            pltpu.VMEM((2, 2, SIDE, part_rows, width), bf16),
            pltpu.VMEM((2, 2, SIDE, part_rows, width), bf16),
            pltpu.VMEM((2, SIDE, part_rows, width), f32),
            pltpu.VMEM((2, 2, part_half, width), bf16),
            pltpu.VMEM((2, 2, part_half, width), bf16),
            pltpu.VMEM((2, 2, part_rows, width), bf16),
            pltpu.VMEM((2, 2, part_rows, width), bf16),
            pltpu.VMEM((rows, 2 * heads_width), f32),
            pltpu.VMEM((rows, 128), f32),
            pltpu.VMEM((question_tokens, 3 * heads_width), f32),
            pltpu.VMEM((question_tokens, 128), f32),
            pltpu.VMEM((requests, tokens, heads_width), bf16),
            pltpu.VMEM((requests, tokens, heads_width), bf16),
            sem((4,)),
            sem((3,)),
            sem,
            sem((n_dp,)),
            sem((n_dp,)),
            sem((6,)),
            sem((6,)),
            sem((PIECES, n_dp)),
            sem((PIECES, n_dp)),
            sem((PIECES, 40)),
            sem((PIECES, 40)),
            sem((40,)),
            sem((40,)),
        ],
        compiler_params=pltpu.CompilerParams(
            collective_id=0, has_side_effects=True, vmem_limit_bytes=56 * 1024 * 1024
        ),
        name="attention_sublayer",
    )(
        retrieved,
        location,
        questions.reshape(question_tokens, width),
        memory,
        norm_gain.reshape(1, n_tp * width),
        w_query.reshape(n_tp, width, heads_width),
        w_key.reshape(n_tp, width, heads_width),
        w_value.reshape(n_tp, width, heads_width),
        w_out,
    )
    return updated[None]


def solution(mesh):
    placed = (
        P("dp", None, "tensor"),
        P("dp", None, "tensor"),
        P("dp", None),
        P(),
        P(),
        P(None, "tensor"),
        P(None, "tensor"),
        P(None, "tensor"),
        P("tensor", None),
    )
    return jax.shard_map(
        on_device,
        mesh=mesh,
        in_specs=placed,
        out_specs=P("dp", None, None, "tensor"),
        check_vma=False,
    )
```

```python
import functools

import jax
import jax.numpy as jnp
from jax import lax
from jax.experimental import pallas as pl
from jax.experimental.pallas import tpu as pltpu
from jax.sharding import PartitionSpec as P

HEAD_DIM = 64
SIDE = 4
PIECES = 4
SLOTS = 2
epsilon = 1e-06
MESH = pl.DeviceIdType.MESH
f32 = jnp.float32
bf16 = jnp.bfloat16


def attend_kernel(
    n_dp,
    n_tp,
    retrieved_ref,
    location_ref,
    questions_hbm,
    memory_hbm,
    gain_hbm,
    wq_hbm,
    wk_hbm,
    wv_hbm,
    wo_hbm,
    updated_ref,
    questions_ref,
    memory_ref,
    gain_ref,
    table,
    tables,
    tables_s,
    place_s,
    outbox,
    held_kv,
    outbox_kv,
    inbox_kv,
    inbox1,
    inbox2,
    inbox3,
    gathered,
    asked,
    wq,
    wkv,
    wo,
    contexts,
    far_out,
    far_in,
    near_out,
    near_in,
    line_sum,
    last_far_out,
    last_far_in,
    last_near_out,
    last_near_in,
    total,
    squares,
    asked_total,
    asked_squares,
    keys,
    values,
    w_sem,
    in_sem,
    tables_sem,
    table_send,
    table_recv,
    asked_send,
    asked_recv,
    fetch_send,
    fetch_recv,
    kv_send,
    kv_recv,
    ring_send,
    ring_recv,
    sum_send,
    sum_recv,
):
    inboxes = (None, inbox1, inbox2, inbox3)
    held, tokens, width = memory_ref.shape
    question_tokens = questions_ref.shape[0]
    requests = retrieved_ref.shape[1]
    piece = tokens // PIECES
    full_width = n_tp * width

    def rows_of(c):
        return (held if c == 0 else requests) * piece

    heads = width // HEAD_DIM
    d = lax.axis_index("dp")
    t = lax.axis_index("tensor")
    x, y = lax.rem(t, SIDE), lax.div(t, SIDE)

    def gain(s):
        return gain_ref[:, pl.ds(pl.multiple_of(s * width, 128), width)]

    def at(dx, dy):
        return lax.rem(y + dy + SIDE, SIDE) * SIDE + lax.rem(x + dx + SIDE, SIDE)

    in_copies = [
        pltpu.make_async_copy(memory_hbm, memory_ref, in_sem.at[0]),
        pltpu.make_async_copy(questions_hbm, questions_ref, in_sem.at[1]),
        pltpu.make_async_copy(gain_hbm, gain_ref, in_sem.at[2]),
    ]
    for copy in in_copies:
        copy.start()

    w_copies = [
        pltpu.make_async_copy(wq_hbm, wq, w_sem.at[0]),
        pltpu.make_async_copy(wk_hbm, wkv.at[:, :, pl.ds(0, width)], w_sem.at[1]),
        pltpu.make_async_copy(wv_hbm, wkv.at[:, :, pl.ds(width, width)], w_sem.at[2]),
        pltpu.make_async_copy(wo_hbm, wo, w_sem.at[3]),
    ]
    for copy in w_copies:
        copy.start()

    barrier = pltpu.get_barrier_semaphore()

    @pl.loop(1, n_dp)
    def _(k):
        pl.semaphore_signal(barrier, inc=1, device_id={"dp": lax.rem(d + k, n_dp)}, device_id_type=MESH)

    for k in range(1, SIDE):
        pl.semaphore_signal(barrier, inc=1, device_id={"tensor": at(k, 0)}, device_id_type=MESH)
        pl.semaphore_signal(barrier, inc=1, device_id={"tensor": at(0, k)}, device_id_type=MESH)

    stored = [location_ref[retrieved_ref[0, j]] for j in range(requests)]
    owners = [s // held for s in stored]
    local = [s % held for s in stored]
    lane = lax.broadcasted_iota(jnp.int32, (8, 128), 1)
    first = jnp.zeros((8, 128), jnp.int32)
    last = jnp.zeros((8, 128), jnp.int32)
    for j in range(requests):
        last = jnp.where(lane == owners[j], local[j], last)
    for j in reversed(range(requests)):
        first = jnp.where(lane == owners[j], local[j], first)
    sub = lax.broadcasted_iota(jnp.int32, (8, 128), 0)
    table[...] = jnp.where(sub == 0, first, last)
    for j in range(requests):
        again = jnp.int32(0)
        for i in range(j):
            again = jnp.where(owners[i] == owners[j], jnp.int32(1), again)
        place_s[j] = owners[j] * SLOTS + again

    tables[pl.ds(d, 1)] = table[...][None]
    in_copies[1].wait()
    asked[pl.ds(t, 1)] = questions_ref[...][None]

    pl.semaphore_wait(barrier, n_dp - 1 + 2 * (SIDE - 1))

    def table_copy(k):
        return pltpu.make_async_remote_copy(
            src_ref=table,
            dst_ref=tables.at[d],
            send_sem=table_send.at[k],
            recv_sem=table_recv.at[k],
            device_id={"dp": lax.rem(d + k, n_dp)},
            device_id_type=MESH,
        )

    def asked_copy(level, k, back):
        if level == 0:
            place = asked.at[at(-back, 0)]
            target = at(k, 0)
        else:
            place = asked.at[pl.ds(lax.rem(y - back + SIDE, SIDE) * SIDE, SIDE)]
            target = at(0, k)
        return pltpu.make_async_remote_copy(
            src_ref=place,
            dst_ref=place,
            send_sem=asked_send.at[level * 3 + k - 1],
            recv_sem=asked_recv.at[level * 3 + k - 1],
            device_id={"tensor": target},
            device_id_type=MESH,
        )

    def table_arrival(k):
        return pltpu.make_async_remote_copy(
            src_ref=table,
            dst_ref=tables.at[lax.rem(d + n_dp - k, n_dp)],
            send_sem=table_send.at[k],
            recv_sem=table_recv.at[k],
            device_id={"dp": lax.rem(d + k, n_dp)},
            device_id_type=MESH,
        )

    def fetch_copy(c, k, sender):
        return pltpu.make_async_remote_copy(
            src_ref=outbox.at[c - 1, k],
            dst_ref=inboxes[c].at[pl.ds(sender * SLOTS, SLOTS)],
            send_sem=fetch_send.at[c, k],
            recv_sem=fetch_recv.at[c, k],
            device_id={"dp": lax.rem(d + k, n_dp)},
            device_id_type=MESH,
        )

    def kv_copy(k, sender):
        return pltpu.make_async_remote_copy(
            src_ref=outbox_kv.at[k],
            dst_ref=inbox_kv.at[pl.ds(sender * SLOTS, SLOTS)],
            send_sem=kv_send.at[k],
            recv_sem=kv_recv.at[k],
            device_id={"dp": lax.rem(d + k, n_dp)},
            device_id_type=MESH,
        )

    def read_tables():
        @pl.loop(1, n_dp)
        def _(k):
            table_arrival(k).wait_recv()

        to_scalar = pltpu.make_async_copy(tables, tables_s, tables_sem)
        to_scalar.start()
        to_scalar.wait()

    def send_pieces(c):
        span = pl.ds(c * piece, piece)

        @pl.loop(1, n_dp)
        def _(k):
            asker = lax.rem(d + k, n_dp)
            for s in range(SLOTS):
                outbox[c - 1, k, s] = memory_ref[tables_s[asker, s, d], span, :]
            fetch_copy(c, k, d).start()

        for s in range(SLOTS):
            inboxes[c][pl.ds(d * SLOTS + s, 1)] = memory_ref[tables_s[d, s, d], span, :][None]

    def send_kv():
        @pl.loop(1, n_dp)
        def _(k):
            asker = lax.rem(d + k, n_dp)
            for s in range(SLOTS):
                outbox_kv[k, s] = held_kv[tables_s[asker, s, d]]
            kv_copy(k, d).start()

        for s in range(SLOTS):
            inbox_kv[pl.ds(d * SLOTS + s, 1)] = held_kv[tables_s[d, s, d]][None]

    def take_kv():
        @pl.loop(1, n_dp)
        def _(k):
            kv_copy(k, lax.rem(d + n_dp - k, n_dp)).wait_recv()

        for j in range(requests):
            both = inbox_kv[place_s[j]]
            keys[j, :piece] = both[:, :width]
            values[j, :piece] = both[:, width:]

    def ring(c, kind, h, direction, k, arrival):
        sign = 1 if direction == 0 else -1
        mine = 0 if not arrival else -sign
        if kind in ("own", "pass"):
            step = (sign, 0) if h == 0 else (0, sign)
            back = (mine, 0) if h == 0 else (0, mine)
            if kind == "own":
                origin = at(*back)
            else:
                origin = at(*(tuple(b - s for b, s in zip(back, step))))
            index = {"own": 0, "pass": 2}[kind] + direction
        else:
            step = (0, sign) if h == 0 else (sign, 0)
            back = (0, mine) if h == 0 else (mine, 0)
            if kind == "turnpass":
                back = tuple(b - s for b, s in zip(back, step))
            shift = (k, 0) if h == 0 else (0, k)
            origin = at(*(b + s for b, s in zip(back, shift)))
            index = {"turn": 4, "turnpass": 12}[kind] + direction * 4 + k % 4
        half = rows_of(c) // 2
        quarter = half // 2
        if kind in ("pass", "turnpass"):
            span = pl.ds(h * half + direction * quarter, quarter)
        else:
            span = pl.ds(h * half, half)
        place = gathered.at[c, origin, span]
        return pltpu.make_async_remote_copy(
            src_ref=place,
            dst_ref=place,
            send_sem=ring_send.at[c, h * 20 + index],
            recv_sem=ring_recv.at[c, h * 20 + index],
            device_id={"tensor": at(*step)},
            device_id_type=MESH,
        )

    def begin(c):
        if c == 0:
            gathered[0, pl.ds(t, 1)] = memory_ref[:, :piece, :].reshape(1, held * piece, width)
        else:

            @pl.loop(1, n_dp)
            def _(k):
                fetch_copy(c, k, lax.rem(d + n_dp - k, n_dp)).wait_recv()

            for j in range(requests):
                gathered[c, pl.ds(t, 1), j * piece : (j + 1) * piece] = inboxes[c][place_s[j]][None]
        for h in range(2):
            for direction in range(2):
                ring(c, "own", h, direction, 0, False).start()

    def along(c):
        for direction in range(2):
            for h in range(2):
                ring(c, "own", h, direction, 0, True).wait_recv()
                ring(c, "pass", h, direction, 0, False).start()

    def turn(c, k):
        for h in range(2):
            if k == 2:
                for direction in range(2):
                    ring(c, "pass", h, direction, 0, True).wait_recv()
            for direction in range(2):
                ring(c, "turn", h, direction, k, False).start()

    def turn_arrivals(c, k):
        for direction in range(2):
            for h in range(2):
                ring(c, "turn", h, direction, k, True).wait_recv()
                ring(c, "turnpass", h, direction, k, False).start()

    def last_arrivals(c):
        for k in (0, -1, 1, 2):
            for direction in range(2):
                for h in range(2):
                    ring(c, "turnpass", h, direction, k, True).wait_recv()

    def multiply(c, s):
        rows = rows_of(c)
        wide = gathered[c, s, :rows].astype(f32)
        normed = (wide * gain(s)).astype(bf16)
        squared = wide * wide
        folded = squared[:, :128]
        for part in range(1, width // 128):
            folded = folded + squared[:, part * 128 : (part + 1) * 128]
        squares[:rows] += folded
        total[:rows] += jnp.dot(normed, wkv[s], preferred_element_type=f32)

    def multiply_range(c, low, high):
        @pl.loop(low, high)
        def _(s):
            multiply(c, s)

    def clear():
        total[...] = jnp.zeros_like(total)
        squares[...] = jnp.zeros_like(squares)

    def finish(c):
        rows = rows_of(c)
        scale = lax.rsqrt(jnp.sum(squares[:rows], axis=1, keepdims=True) / full_width + epsilon)
        if c == 0:
            held_kv[...] = (total[:rows] * scale).astype(bf16).reshape(held, piece, 2 * width)
        else:
            span = pl.ds(c * piece, piece)
            key = (total[:rows, :width] * scale).astype(bf16)
            keys[:, span, :] = key.reshape(requests, piece, width)
            value = (total[:rows, width:] * scale).astype(bf16)
            values[:, span, :] = value.reshape(requests, piece, width)

    def ask():
        for copy in w_copies:
            copy.wait()

        in_copies[2].wait()
        for k in range(1, SIDE):
            asked_copy(1, k, k).wait_recv()

        asked_total[...] = jnp.zeros_like(asked_total)
        asked_squares[...] = jnp.zeros_like(asked_squares)

        @pl.loop(0, n_tp)
        def _(s):
            wide = asked[s].astype(f32)
            normed = (wide * gain(s)).astype(bf16)
            asked_squares[...] += jnp.sum(wide * wide, axis=1, keepdims=True)
            asked_total[:, :width] += jnp.dot(normed, wq[s], preferred_element_type=f32)
            asked_total[:, width:] += jnp.dot(normed, wkv[s], preferred_element_type=f32)

    quarter_tp = n_tp // 4
    last_piece = PIECES - 1
    shifts = (0, -1, 1, 2)

    @pl.loop(1, n_dp)
    def _(k):
        table_copy(k).start()

    in_copies[0].wait()
    begin(0)
    for k in range(1, SIDE):
        asked_copy(0, k, 0).start()
    along(0)
    for k in (0, -1, 1):
        turn(0, k)
    read_tables()
    send_pieces(1)
    turn(0, 2)
    send_pieces(2)
    for k in range(1, SIDE):
        asked_copy(0, k, k).wait_recv()
    for k in range(1, SIDE):
        asked_copy(1, k, 0).start()
    send_pieces(3)
    turn_arrivals(0, 0)
    ask()
    for k in (-1, 1, 2):
        turn_arrivals(0, k)
    begin(1)
    for c in range(1, PIECES):
        along(c)
        for k in (0, -1, 1):
            turn(c, k)
        if c < last_piece:
            begin(c + 1)
        turn(c, 2)
        if c == 1:
            last_arrivals(0)
            clear()
            multiply_range(0, 0, n_tp)
            finish(0)
            send_kv()
        if c > 2:
            last_arrivals(c - 2)
            clear()
        for i, k in enumerate(shifts):
            if c > 1:
                turn_arrivals(c - 1, k)
            if c > 2:
                multiply_range(c - 2, i * quarter_tp, (i + 1) * quarter_tp)
        if c > 2:
            finish(c - 2)
    last_arrivals(last_piece - 1)
    clear()
    for i, k in enumerate((0, -1, 1, 2)):
        turn_arrivals(last_piece, k)
        multiply_range(last_piece - 1, i * quarter_tp, (i + 1) * quarter_tp)
    finish(last_piece - 1)
    clear()

    @pl.loop(0, 9)
    def _(i):
        multiply(last_piece, at(lax.rem(i, 3) - 1, lax.div(i, 3) - 1))

    last_arrivals(last_piece)

    @pl.loop(0, 7)
    def _(i):
        multiply(last_piece, at(lax.select(i < 4, 2, i - 5), lax.select(i < 4, i - 1, 2)))

    finish(last_piece)

    asked_scale = lax.rsqrt(asked_squares[:, :1] / full_width + epsilon)
    projected = (asked_total[...] * asked_scale).astype(bf16)
    own_query = projected[:, :width] * jnp.asarray(HEAD_DIM ** (-0.5), bf16)
    own_key = projected[:, width : 2 * width]
    own_value = projected[:, 2 * width :]
    head_of = lax.broadcasted_iota(jnp.int32, (question_tokens, width), 1) // HEAD_DIM
    spread = jnp.concatenate(
        [jnp.where(head_of == h, own_query, jnp.zeros_like(own_query)) for h in range(heads)], axis=0
    )

    def dot_t(a, b):
        return lax.dot_general(a, b, (((1,), (1,)), ((), ())), preferred_element_type=f32)

    own_scores = dot_t(spread, own_key)
    own_most = jnp.max(own_scores, axis=1, keepdims=True)

    take_kv()

    def attend(j):
        scores = dot_t(spread, keys[j])
        most = jnp.maximum(own_most, jnp.max(scores, axis=1, keepdims=True))
        far = jnp.exp(scores - most)
        own = jnp.exp(own_scores - most)
        mass = jnp.sum(far, axis=1, keepdims=True) + jnp.sum(own, axis=1, keepdims=True)
        share = 1.0 / mass
        out = jnp.dot((far * share).astype(bf16), values[j], preferred_element_type=f32)
        out += jnp.dot((own * share).astype(bf16), own_value, preferred_element_type=f32)
        context = jnp.zeros((question_tokens, width), f32)
        for h in range(heads):
            block = out[h * question_tokens : (h + 1) * question_tokens]
            context = context + jnp.where(head_of == h, block, jnp.zeros_like(block))
        contexts[j] = context.astype(bf16)

    part = requests // 2
    part_rows = part * question_tokens
    part_half = part_rows // 2

    def aim(h, k1, k2):
        return at(k1, k2) if h == 0 else at(k2, k1)

    def term(h, low, count, s):
        rows_in = contexts[h * part : (h + 1) * part].reshape(part_rows, width)[low : low + count]
        columns = wo[:, pl.ds(pl.multiple_of(s * width, 128), width)]
        return jnp.dot(rows_in, columns, preferred_element_type=f32)

    def hop(kind, h, direction, k):
        sign = 1 if direction == 0 else -1
        k = k % 4
        if kind == "far":
            src, dst, index = far_out.at[h, direction, k], far_in.at[h, direction, k], direction * 4 + k
        elif kind == "near":
            src, dst, index = near_out.at[h, direction, k], near_in.at[h, direction, k], 8 + direction * 4 + k
        elif kind == "last_far":
            src, dst, index = last_far_out.at[h, direction], last_far_in.at[h, direction], 16 + direction
        else:
            src, dst, index = last_near_out.at[h, direction], last_near_in.at[h, direction], 18 + direction
        target = aim(h, sign, 0) if kind in ("far", "near") else aim(h, 0, sign)
        return pltpu.make_async_remote_copy(
            src_ref=src,
            dst_ref=dst,
            send_sem=sum_send.at[h * 20 + index],
            recv_sem=sum_recv.at[h * 20 + index],
            device_id={"tensor": target},
            device_id_type=MESH,
        )

    order = (2, 1, -1, 0)

    def send_far(h):
        for k in order:
            for direction in range(2):
                far_out[h, direction, k % 4] = term(h, direction * part_half, part_half, aim(h, 2, k)).astype(bf16)
                hop("far", h, direction, k).start()

    def send_near(h, k):
        for direction in range(2):
            sign = 1 if direction == 0 else -1
            low = direction * part_half
            here = term(h, 0, part_rows, aim(h, sign, k))
            hop("far", h, direction, k).wait_recv()
            passed = here[low : low + part_half] + far_in[h, direction, k % 4].astype(f32)
            other = part_half - low
            near_out[h, direction, k % 4, low : low + part_half] = passed.astype(bf16)
            near_out[h, direction, k % 4, other : other + part_half] = here[other : other + part_half].astype(bf16)
            hop("near", h, direction, k).start()

    def sum_line(h, k):
        here = term(h, 0, part_rows, aim(h, 0, k))
        for direction in range(2):
            hop("near", h, direction, k).wait_recv()
            here = here + near_in[h, direction, k % 4].astype(f32)
        line_sum[h, k % 4] = here

    def send_last_far(h):
        for direction in range(2):
            low = direction * part_half
            last_far_out[h, direction] = line_sum[h, 2, low : low + part_half].astype(bf16)
            hop("last_far", h, direction, 0).start()

    def send_last_near(h):
        for direction in range(2):
            k = 1 if direction == 0 else 3
            low = direction * part_half
            other = part_half - low
            hop("last_far", h, direction, 0).wait_recv()
            passed = line_sum[h, k, low : low + part_half] + last_far_in[h, direction].astype(f32)
            last_near_out[h, direction, low : low + part_half] = passed.astype(bf16)
            last_near_out[h, direction, other : other + part_half] = line_sum[h, k, other : other + part_half].astype(bf16)
            hop("last_near", h, direction, 0).start()

    def settle(h):
        summed = line_sum[h, 0]
        for direction in range(2):
            hop("last_near", h, direction, 0).wait_recv()
            summed = summed + last_near_in[h, direction].astype(f32)
        summed = summed.reshape(part, question_tokens, width)
        updated_ref[h * part : (h + 1) * part] = (questions_ref[...].astype(f32)[None] + summed).astype(bf16)

    for h in range(2):

        for j in range(h * part, (h + 1) * part):
            attend(j)

        send_far(h)
    for k in order:
        for h in range(2):
            send_near(h, k)
    for k in order:
        for h in range(2):
            sum_line(h, k)
            if k == 2:
                send_last_far(h)
            if k == -1:
                send_last_near(h)
    for h in range(2):
        settle(h)

    @pl.loop(1, n_dp)
    def _(k):
        table_copy(k).wait_send()
        for c in range(1, PIECES):
            fetch_copy(c, k, d).wait_send()
        kv_copy(k, d).wait_send()

    for level in range(2):
        for k in range(1, SIDE):
            asked_copy(level, k, 0).wait_send()

    for c in range(PIECES):
        for h in range(2):
            for direction in range(2):
                for kind in ("own", "pass"):
                    ring(c, kind, h, direction, 0, False).wait_send()
                for k in range(4):
                    for kind in ("turn", "turnpass"):
                        ring(c, kind, h, direction, k, False).wait_send()

    for h in range(2):
        for direction in range(2):
            for k in range(4):
                for kind in ("far", "near"):
                    hop(kind, h, direction, k).wait_send()
            for kind in ("last_far", "last_near"):
                hop(kind, h, direction, 0).wait_send()


def on_device(questions, memory, retrieved, location, norm_gain, w_query, w_key, w_value, w_out):
    n_dp, n_tp = lax.axis_size("dp"), lax.axis_size("tensor")
    question_count, question_tokens, width = questions.shape
    held, tokens, _ = memory.shape
    requests = retrieved.shape[1]
    heads_width = w_key.shape[1]
    piece = tokens // PIECES
    rows = max(held, requests) * piece
    part_rows = (requests // 2) * question_tokens
    part_half = part_rows // 2
    sem = pltpu.SemaphoreType.DMA
    vmem = pl.BlockSpec(memory_space=pltpu.VMEM)
    smem = pl.BlockSpec(memory_space=pltpu.SMEM)
    hbm = pl.BlockSpec(memory_space=pl.ANY)
    updated = pl.pallas_call(
        functools.partial(attend_kernel, n_dp, n_tp),
        out_shape=jax.ShapeDtypeStruct((requests, question_tokens, width), bf16),
        in_specs=[smem, smem] + [hbm] * 7,
        out_specs=vmem,
        scratch_shapes=[
            pltpu.VMEM((question_tokens, width), bf16),
            pltpu.VMEM((held, tokens, width), bf16),
            pltpu.VMEM((1, n_tp * width), f32),
            pltpu.VMEM((8, 128), jnp.int32),
            pltpu.VMEM((n_dp, 8, 128), jnp.int32),
            pltpu.SMEM((n_dp, 8, 128), jnp.int32),
            pltpu.SMEM((requests,), jnp.int32),
            pltpu.VMEM((PIECES - 1, n_dp, SLOTS, piece, width), bf16),
            pltpu.VMEM((held, piece, 2 * heads_width), bf16),
            pltpu.VMEM((n_dp, SLOTS, piece, 2 * heads_width), bf16),
            pltpu.VMEM((n_dp * SLOTS, piece, 2 * heads_width), bf16),
            pltpu.VMEM((n_dp * SLOTS, piece, width), bf16),
            pltpu.VMEM((n_dp * SLOTS, piece, width), bf16),
            pltpu.VMEM((n_dp * SLOTS, piece, width), bf16),
            pltpu.VMEM((PIECES, n_tp, rows, width), bf16),
            pltpu.VMEM((n_tp, question_tokens, width), bf16),
            pltpu.VMEM((n_tp, width, heads_width), bf16),
            pltpu.VMEM((n_tp, width, 2 * heads_width), bf16),
            pltpu.VMEM((heads_width, n_tp * width), bf16),
            pltpu.VMEM((requests, question_tokens, heads_width), bf16),
            pltpu.VMEM((2, 2, SIDE, part_half, width), bf16),
            pltpu.VMEM((2, 2, SIDE, part_half, width), bf16),
            pltpu.VMEM((2, 2, SIDE, part_rows, width), bf16),
            pltpu.VMEM((2, 2, SIDE, part_rows, width), bf16),
            pltpu.VMEM((2, SIDE, part_rows, width), f32),
            pltpu.VMEM((2, 2, part_half, width), bf16),
            pltpu.VMEM((2, 2, part_half, width), bf16),
            pltpu.VMEM((2, 2, part_rows, width), bf16),
            pltpu.VMEM((2, 2, part_rows, width), bf16),
            pltpu.VMEM((rows, 2 * heads_width), f32),
            pltpu.VMEM((rows, 128), f32),
            pltpu.VMEM((question_tokens, 3 * heads_width), f32),
            pltpu.VMEM((question_tokens, 128), f32),
            pltpu.VMEM((requests, tokens, heads_width), bf16),
            pltpu.VMEM((requests, tokens, heads_width), bf16),
            sem((4,)),
            sem((3,)),
            sem,
            sem((n_dp,)),
            sem((n_dp,)),
            sem((6,)),
            sem((6,)),
            sem((PIECES, n_dp)),
            sem((PIECES, n_dp)),
            sem((n_dp,)),
            sem((n_dp,)),
            sem((PIECES, 40)),
            sem((PIECES, 40)),
            sem((40,)),
            sem((40,)),
        ],
        compiler_params=pltpu.CompilerParams(
            collective_id=0, has_side_effects=True, vmem_limit_bytes=56 * 1024 * 1024
        ),
        name="attention_sublayer",
    )(
        retrieved,
        location,
        questions.reshape(question_tokens, width),
        memory,
        norm_gain.reshape(1, n_tp * width),
        w_query.reshape(n_tp, width, heads_width),
        w_key.reshape(n_tp, width, heads_width),
        w_value.reshape(n_tp, width, heads_width),
        w_out,
    )
    return updated[None]


def solution(mesh):
    placed = (
        P("dp", None, "tensor"),
        P("dp", None, "tensor"),
        P("dp", None),
        P(),
        P(),
        P(None, "tensor"),
        P(None, "tensor"),
        P(None, "tensor"),
        P("tensor", None),
    )
    return jax.shard_map(
        on_device,
        mesh=mesh,
        in_specs=placed,
        out_specs=P("dp", None, None, "tensor"),
        check_vma=False,
    )
```

```python
import functools

import jax
import jax.numpy as jnp
from jax import lax
from jax.experimental import pallas as pl
from jax.experimental.pallas import tpu as pltpu
from jax.sharding import PartitionSpec as P

HEAD_DIM = 64
SIDE = 4
PIECES = 4
SLOTS = 2
epsilon = 1e-06
MESH = pl.DeviceIdType.MESH
f32 = jnp.float32
bf16 = jnp.bfloat16


def attend_kernel(
    n_dp,
    n_tp,
    retrieved_ref,
    location_ref,
    questions_hbm,
    memory_hbm,
    gain_hbm,
    wq_hbm,
    wk_hbm,
    wv_hbm,
    wo_hbm,
    updated_ref,
    questions_ref,
    memory_ref,
    gain_ref,
    table,
    tables,
    tables_s,
    place_s,
    outbox,
    held_kv,
    outbox_kv,
    inbox_kv,
    inbox1,
    inbox2,
    inbox3,
    gathered,
    asked,
    wq,
    wkv,
    wo,
    contexts,
    far_out,
    far_in,
    near_out,
    near_in,
    line_sum,
    last_far_out,
    last_far_in,
    last_near_out,
    last_near_in,
    total,
    squares,
    asked_total,
    asked_squares,
    keys,
    values,
    w_sem,
    in_sem,
    tables_sem,
    table_send,
    table_recv,
    asked_send,
    asked_recv,
    fetch_send,
    fetch_recv,
    kv_send,
    kv_recv,
    ring_send,
    ring_recv,
    sum_send,
    sum_recv,
):
    inboxes = (None, inbox1, inbox2, inbox3)
    held, tokens, width = memory_ref.shape
    question_tokens = questions_ref.shape[0]
    requests = retrieved_ref.shape[1]
    piece = tokens // PIECES
    full_width = n_tp * width

    def rows_of(c):
        return (held if c == 0 else requests) * piece

    heads = width // HEAD_DIM
    d = lax.axis_index("dp")
    t = lax.axis_index("tensor")
    x, y = lax.rem(t, SIDE), lax.div(t, SIDE)

    def gain(s):
        return gain_ref[:, pl.ds(pl.multiple_of(s * width, 128), width)]

    def at(dx, dy):
        return lax.rem(y + dy + SIDE, SIDE) * SIDE + lax.rem(x + dx + SIDE, SIDE)

    in_copies = [
        pltpu.make_async_copy(memory_hbm, memory_ref, in_sem.at[0]),
        pltpu.make_async_copy(questions_hbm, questions_ref, in_sem.at[1]),
        pltpu.make_async_copy(gain_hbm, gain_ref, in_sem.at[2]),
    ]
    for copy in in_copies:
        copy.start()

    w_copies = [
        pltpu.make_async_copy(wq_hbm, wq, w_sem.at[0]),
        pltpu.make_async_copy(wk_hbm, wkv.at[:, :, pl.ds(0, width)], w_sem.at[1]),
        pltpu.make_async_copy(wv_hbm, wkv.at[:, :, pl.ds(width, width)], w_sem.at[2]),
        pltpu.make_async_copy(wo_hbm, wo, w_sem.at[3]),
    ]
    for copy in w_copies:
        copy.start()

    barrier = pltpu.get_barrier_semaphore()

    @pl.loop(1, n_dp)
    def _(k):
        pl.semaphore_signal(barrier, inc=1, device_id={"dp": lax.rem(d + k, n_dp)}, device_id_type=MESH)

    for k in range(1, SIDE):
        pl.semaphore_signal(barrier, inc=1, device_id={"tensor": at(k, 0)}, device_id_type=MESH)
        pl.semaphore_signal(barrier, inc=1, device_id={"tensor": at(0, k)}, device_id_type=MESH)

    stored = [location_ref[retrieved_ref[0, j]] for j in range(requests)]
    owners = [s // held for s in stored]
    local = [s % held for s in stored]
    lane = lax.broadcasted_iota(jnp.int32, (8, 128), 1)
    first = jnp.zeros((8, 128), jnp.int32)
    last = jnp.zeros((8, 128), jnp.int32)
    for j in range(requests):
        last = jnp.where(lane == owners[j], local[j], last)
    for j in reversed(range(requests)):
        first = jnp.where(lane == owners[j], local[j], first)
    sub = lax.broadcasted_iota(jnp.int32, (8, 128), 0)
    table[...] = jnp.where(sub == 0, first, last)
    for j in range(requests):
        again = jnp.int32(0)
        for i in range(j):
            again = jnp.where(owners[i] == owners[j], jnp.int32(1), again)
        place_s[j] = owners[j] * SLOTS + again

    tables[pl.ds(d, 1)] = table[...][None]
    in_copies[1].wait()
    asked[pl.ds(t, 1)] = questions_ref[...][None]

    pl.semaphore_wait(barrier, n_dp - 1 + 2 * (SIDE - 1))

    def table_copy(k):
        return pltpu.make_async_remote_copy(
            src_ref=table,
            dst_ref=tables.at[d],
            send_sem=table_send.at[k],
            recv_sem=table_recv.at[k],
            device_id={"dp": lax.rem(d + k, n_dp)},
            device_id_type=MESH,
        )

    def asked_copy(level, k, back):
        if level == 0:
            place = asked.at[at(-back, 0)]
            target = at(k, 0)
        else:
            place = asked.at[pl.ds(lax.rem(y - back + SIDE, SIDE) * SIDE, SIDE)]
            target = at(0, k)
        return pltpu.make_async_remote_copy(
            src_ref=place,
            dst_ref=place,
            send_sem=asked_send.at[level * 3 + k - 1],
            recv_sem=asked_recv.at[level * 3 + k - 1],
            device_id={"tensor": target},
            device_id_type=MESH,
        )

    def table_arrival(k):
        return pltpu.make_async_remote_copy(
            src_ref=table,
            dst_ref=tables.at[lax.rem(d + n_dp - k, n_dp)],
            send_sem=table_send.at[k],
            recv_sem=table_recv.at[k],
            device_id={"dp": lax.rem(d + k, n_dp)},
            device_id_type=MESH,
        )

    def fetch_copy(c, k, sender):
        return pltpu.make_async_remote_copy(
            src_ref=outbox.at[c - 1, k],
            dst_ref=inboxes[c].at[pl.ds(sender * SLOTS, SLOTS)],
            send_sem=fetch_send.at[c, k],
            recv_sem=fetch_recv.at[c, k],
            device_id={"dp": lax.rem(d + k, n_dp)},
            device_id_type=MESH,
        )

    def kv_copy(k, sender):
        return pltpu.make_async_remote_copy(
            src_ref=outbox_kv.at[k],
            dst_ref=inbox_kv.at[pl.ds(sender * SLOTS, SLOTS)],
            send_sem=kv_send.at[k],
            recv_sem=kv_recv.at[k],
            device_id={"dp": lax.rem(d + k, n_dp)},
            device_id_type=MESH,
        )

    def read_tables():
        @pl.loop(1, n_dp)
        def _(k):
            table_arrival(k).wait_recv()

        to_scalar = pltpu.make_async_copy(tables, tables_s, tables_sem)
        to_scalar.start()
        to_scalar.wait()

    def send_pieces(c):
        span = pl.ds(c * piece, piece)

        @pl.loop(1, n_dp)
        def _(k):
            asker = lax.rem(d + k, n_dp)
            for s in range(SLOTS):
                outbox[c - 1, k, s] = memory_ref[tables_s[asker, s, d], span, :]
            fetch_copy(c, k, d).start()

        for s in range(SLOTS):
            inboxes[c][pl.ds(d * SLOTS + s, 1)] = memory_ref[tables_s[d, s, d], span, :][None]

    def send_kv():
        @pl.loop(1, n_dp)
        def _(k):
            asker = lax.rem(d + k, n_dp)
            for s in range(SLOTS):
                outbox_kv[k, s] = held_kv[tables_s[asker, s, d]]
            kv_copy(k, d).start()

        for s in range(SLOTS):
            inbox_kv[pl.ds(d * SLOTS + s, 1)] = held_kv[tables_s[d, s, d]][None]

    def take_kv():
        @pl.loop(1, n_dp)
        def _(k):
            kv_copy(k, lax.rem(d + n_dp - k, n_dp)).wait_recv()

        for j in range(requests):
            both = inbox_kv[place_s[j]]
            keys[j, :piece] = both[:, :width]
            values[j, :piece] = both[:, width:]

    def ring(c, kind, h, direction, k, arrival):
        sign = 1 if direction == 0 else -1
        mine = 0 if not arrival else -sign
        if kind in ("own", "pass"):
            step = (sign, 0) if h == 0 else (0, sign)
            back = (mine, 0) if h == 0 else (0, mine)
            if kind == "own":
                origin = at(*back)
            else:
                origin = at(*(tuple(b - s for b, s in zip(back, step))))
            index = {"own": 0, "pass": 2}[kind] + direction
        else:
            step = (0, sign) if h == 0 else (sign, 0)
            back = (0, mine) if h == 0 else (mine, 0)
            if kind == "turnpass":
                back = tuple(b - s for b, s in zip(back, step))
            shift = (k, 0) if h == 0 else (0, k)
            origin = at(*(b + s for b, s in zip(back, shift)))
            index = {"turn": 4, "turnpass": 12}[kind] + direction * 4 + k % 4
        half = rows_of(c) // 2
        quarter = half // 2
        if kind in ("pass", "turnpass"):
            span = pl.ds(h * half + direction * quarter, quarter)
        else:
            span = pl.ds(h * half, half)
        place = gathered.at[c, origin, span]
        return pltpu.make_async_remote_copy(
            src_ref=place,
            dst_ref=place,
            send_sem=ring_send.at[c, h * 20 + index],
            recv_sem=ring_recv.at[c, h * 20 + index],
            device_id={"tensor": at(*step)},
            device_id_type=MESH,
        )

    def begin(c):
        if c == 0:
            gathered[0, pl.ds(t, 1)] = memory_ref[:, :piece, :].reshape(1, held * piece, width)
        else:

            @pl.loop(1, n_dp)
            def _(k):
                fetch_copy(c, k, lax.rem(d + n_dp - k, n_dp)).wait_recv()

            for j in range(requests):
                gathered[c, pl.ds(t, 1), j * piece : (j + 1) * piece] = inboxes[c][place_s[j]][None]
        for h in range(2):
            for direction in range(2):
                ring(c, "own", h, direction, 0, False).start()

    def along(c):
        for direction in range(2):
            for h in range(2):
                ring(c, "own", h, direction, 0, True).wait_recv()
                ring(c, "pass", h, direction, 0, False).start()

    def turn(c, k):
        for h in range(2):
            if k == 2:
                for direction in range(2):
                    ring(c, "pass", h, direction, 0, True).wait_recv()
            for direction in range(2):
                ring(c, "turn", h, direction, k, False).start()

    def turn_arrivals(c, k):
        for direction in range(2):
            for h in range(2):
                ring(c, "turn", h, direction, k, True).wait_recv()
                ring(c, "turnpass", h, direction, k, False).start()

    def last_arrivals(c):
        for k in (0, -1, 1, 2):
            for direction in range(2):
                for h in range(2):
                    ring(c, "turnpass", h, direction, k, True).wait_recv()

    def multiply(c, s):
        rows = rows_of(c)
        wide = gathered[c, s, :rows].astype(f32)
        normed = (wide * gain(s)).astype(bf16)
        squared = wide * wide
        folded = squared[:, :128]
        for part in range(1, width // 128):
            folded = folded + squared[:, part * 128 : (part + 1) * 128]
        squares[:rows] += folded
        total[:rows] += jnp.dot(normed, wkv[s], preferred_element_type=f32)

    def multiply_range(c, low, high):
        @pl.loop(low, high)
        def _(s):
            multiply(c, s)

    def clear():
        total[...] = jnp.zeros_like(total)
        squares[...] = jnp.zeros_like(squares)

    def finish(c):
        rows = rows_of(c)
        scale = lax.rsqrt(jnp.sum(squares[:rows], axis=1, keepdims=True) / full_width + epsilon)
        if c == 0:
            held_kv[...] = (total[:rows] * scale).astype(bf16).reshape(held, piece, 2 * width)
        else:
            span = pl.ds(c * piece, piece)
            key = (total[:rows, :width] * scale).astype(bf16)
            keys[:, span, :] = key.reshape(requests, piece, width)
            value = (total[:rows, width:] * scale).astype(bf16)
            values[:, span, :] = value.reshape(requests, piece, width)

    head_of = lax.broadcasted_iota(jnp.int32, (question_tokens, width), 1) // HEAD_DIM

    def dot_t(a, b):
        return lax.dot_general(a, b, (((1,), (1,)), ((), ())), preferred_element_type=f32)

    def ask():
        for copy in w_copies:
            copy.wait()

        in_copies[2].wait()
        for k in range(1, SIDE):
            asked_copy(1, k, k).wait_recv()

        asked_total[...] = jnp.zeros_like(asked_total)
        asked_squares[...] = jnp.zeros_like(asked_squares)

        @pl.loop(0, n_tp)
        def _(s):
            wide = asked[s].astype(f32)
            normed = (wide * gain(s)).astype(bf16)
            asked_squares[...] += jnp.sum(wide * wide, axis=1, keepdims=True)
            asked_total[:, :width] += jnp.dot(normed, wq[s], preferred_element_type=f32)
            asked_total[:, width:] += jnp.dot(normed, wkv[s], preferred_element_type=f32)

        asked_scale = lax.rsqrt(asked_squares[:, :1] / full_width + epsilon)
        projected = (asked_total[...] * asked_scale).astype(bf16)
        own_query = projected[:, :width] * jnp.asarray(HEAD_DIM ** (-0.5), bf16)
        own_key = projected[:, width : 2 * width]
        own_value = projected[:, 2 * width :]
        spread = jnp.concatenate(
            [jnp.where(head_of == h, own_query, jnp.zeros_like(own_query)) for h in range(heads)], axis=0
        )

        own_scores = dot_t(spread, own_key)
        own_most = jnp.max(own_scores, axis=1, keepdims=True)
        return spread, own_value, own_scores, own_most

    quarter_tp = n_tp // 4
    last_piece = PIECES - 1
    shifts = (0, -1, 1, 2)

    @pl.loop(1, n_dp)
    def _(k):
        table_copy(k).start()

    in_copies[0].wait()
    begin(0)
    for k in range(1, SIDE):
        asked_copy(0, k, 0).start()
    along(0)
    for k in (0, -1, 1):
        turn(0, k)
    read_tables()
    send_pieces(1)
    turn(0, 2)
    send_pieces(2)
    for k in range(1, SIDE):
        asked_copy(0, k, k).wait_recv()
    for k in range(1, SIDE):
        asked_copy(1, k, 0).start()
    send_pieces(3)
    turn_arrivals(0, 0)
    turn_arrivals(0, -1)
    begin(1)
    turn_arrivals(0, 1)
    along(1)
    turn_arrivals(0, 2)
    for k in (0, -1, 1, 2):
        turn(1, k)
    spread, own_value, own_scores, own_most = ask()
    begin(2)
    for c in range(2, PIECES):
        along(c)
        if c < last_piece:
            begin(c + 1)
        last_arrivals(c - 2)
        clear()
        for i, k in enumerate(shifts):
            turn_arrivals(c - 1, k)
            turn(c, k)
            multiply_range(c - 2, i * quarter_tp, (i + 1) * quarter_tp)
        finish(c - 2)
        if c == 2:
            send_kv()
    last_arrivals(last_piece - 1)
    clear()
    for i, k in enumerate((0, -1, 1, 2)):
        turn_arrivals(last_piece, k)
        multiply_range(last_piece - 1, i * quarter_tp, (i + 1) * quarter_tp)
    finish(last_piece - 1)
    clear()

    @pl.loop(0, 9)
    def _(i):
        multiply(last_piece, at(lax.rem(i, 3) - 1, lax.div(i, 3) - 1))

    take_kv()
    last_arrivals(last_piece)

    @pl.loop(0, 7)
    def _(i):
        multiply(last_piece, at(lax.select(i < 4, 2, i - 5), lax.select(i < 4, i - 1, 2)))

    finish(last_piece)

    def attend(j):
        scores = dot_t(spread, keys[j])
        most = jnp.maximum(own_most, jnp.max(scores, axis=1, keepdims=True))
        far = jnp.exp(scores - most)
        own = jnp.exp(own_scores - most)
        mass = jnp.sum(far, axis=1, keepdims=True) + jnp.sum(own, axis=1, keepdims=True)
        share = 1.0 / mass
        out = jnp.dot((far * share).astype(bf16), values[j], preferred_element_type=f32)
        out += jnp.dot((own * share).astype(bf16), own_value, preferred_element_type=f32)
        context = jnp.zeros((question_tokens, width), f32)
        for h in range(heads):
            block = out[h * question_tokens : (h + 1) * question_tokens]
            context = context + jnp.where(head_of == h, block, jnp.zeros_like(block))
        contexts[j] = context.astype(bf16)

    part = requests // 2
    part_rows = part * question_tokens
    part_half = part_rows // 2

    def aim(h, k1, k2):
        return at(k1, k2) if h == 0 else at(k2, k1)

    def term(h, low, count, s):
        rows_in = contexts[h * part : (h + 1) * part].reshape(part_rows, width)[low : low + count]
        columns = wo[:, pl.ds(pl.multiple_of(s * width, 128), width)]
        return jnp.dot(rows_in, columns, preferred_element_type=f32)

    def hop(kind, h, direction, k):
        sign = 1 if direction == 0 else -1
        k = k % 4
        if kind == "far":
            src, dst, index = far_out.at[h, direction, k], far_in.at[h, direction, k], direction * 4 + k
        elif kind == "near":
            src, dst, index = near_out.at[h, direction, k], near_in.at[h, direction, k], 8 + direction * 4 + k
        elif kind == "last_far":
            src, dst, index = last_far_out.at[h, direction], last_far_in.at[h, direction], 16 + direction
        else:
            src, dst, index = last_near_out.at[h, direction], last_near_in.at[h, direction], 18 + direction
        target = aim(h, sign, 0) if kind in ("far", "near") else aim(h, 0, sign)
        return pltpu.make_async_remote_copy(
            src_ref=src,
            dst_ref=dst,
            send_sem=sum_send.at[h * 20 + index],
            recv_sem=sum_recv.at[h * 20 + index],
            device_id={"tensor": target},
            device_id_type=MESH,
        )

    order = (2, 1, -1, 0)

    def send_far(h):
        for k in order:
            for direction in range(2):
                far_out[h, direction, k % 4] = term(h, direction * part_half, part_half, aim(h, 2, k)).astype(bf16)
                hop("far", h, direction, k).start()

    def send_near(h, k):
        for direction in range(2):
            sign = 1 if direction == 0 else -1
            low = direction * part_half
            here = term(h, 0, part_rows, aim(h, sign, k))
            hop("far", h, direction, k).wait_recv()
            passed = here[low : low + part_half] + far_in[h, direction, k % 4].astype(f32)
            other = part_half - low
            near_out[h, direction, k % 4, low : low + part_half] = passed.astype(bf16)
            near_out[h, direction, k % 4, other : other + part_half] = here[other : other + part_half].astype(bf16)
            hop("near", h, direction, k).start()

    def sum_line(h, k):
        here = term(h, 0, part_rows, aim(h, 0, k))
        for direction in range(2):
            hop("near", h, direction, k).wait_recv()
            here = here + near_in[h, direction, k % 4].astype(f32)
        line_sum[h, k % 4] = here

    def send_last_far(h):
        for direction in range(2):
            low = direction * part_half
            last_far_out[h, direction] = line_sum[h, 2, low : low + part_half].astype(bf16)
            hop("last_far", h, direction, 0).start()

    def send_last_near(h):
        for direction in range(2):
            k = 1 if direction == 0 else 3
            low = direction * part_half
            other = part_half - low
            hop("last_far", h, direction, 0).wait_recv()
            passed = line_sum[h, k, low : low + part_half] + last_far_in[h, direction].astype(f32)
            last_near_out[h, direction, low : low + part_half] = passed.astype(bf16)
            last_near_out[h, direction, other : other + part_half] = line_sum[h, k, other : other + part_half].astype(bf16)
            hop("last_near", h, direction, 0).start()

    def settle(h):
        summed = line_sum[h, 0]
        for direction in range(2):
            hop("last_near", h, direction, 0).wait_recv()
            summed = summed + last_near_in[h, direction].astype(f32)
        summed = summed.reshape(part, question_tokens, width)
        updated_ref[h * part : (h + 1) * part] = (questions_ref[...].astype(f32)[None] + summed).astype(bf16)

    for h in range(2):

        for j in range(h * part, (h + 1) * part):
            attend(j)

        send_far(h)
    for k in order:
        for h in range(2):
            send_near(h, k)
    for k in order:
        for h in range(2):
            sum_line(h, k)
            if k == 2:
                send_last_far(h)
            if k == -1:
                send_last_near(h)
    for h in range(2):
        settle(h)

    @pl.loop(1, n_dp)
    def _(k):
        table_copy(k).wait_send()
        for c in range(1, PIECES):
            fetch_copy(c, k, d).wait_send()
        kv_copy(k, d).wait_send()

    for level in range(2):
        for k in range(1, SIDE):
            asked_copy(level, k, 0).wait_send()

    for c in range(PIECES):
        for h in range(2):
            for direction in range(2):
                for kind in ("own", "pass"):
                    ring(c, kind, h, direction, 0, False).wait_send()
                for k in range(4):
                    for kind in ("turn", "turnpass"):
                        ring(c, kind, h, direction, k, False).wait_send()

    for h in range(2):
        for direction in range(2):
            for k in range(4):
                for kind in ("far", "near"):
                    hop(kind, h, direction, k).wait_send()
            for kind in ("last_far", "last_near"):
                hop(kind, h, direction, 0).wait_send()


def on_device(questions, memory, retrieved, location, norm_gain, w_query, w_key, w_value, w_out):
    n_dp, n_tp = lax.axis_size("dp"), lax.axis_size("tensor")
    question_count, question_tokens, width = questions.shape
    held, tokens, _ = memory.shape
    requests = retrieved.shape[1]
    heads_width = w_key.shape[1]
    piece = tokens // PIECES
    rows = max(held, requests) * piece
    part_rows = (requests // 2) * question_tokens
    part_half = part_rows // 2
    sem = pltpu.SemaphoreType.DMA
    vmem = pl.BlockSpec(memory_space=pltpu.VMEM)
    smem = pl.BlockSpec(memory_space=pltpu.SMEM)
    hbm = pl.BlockSpec(memory_space=pl.ANY)
    updated = pl.pallas_call(
        functools.partial(attend_kernel, n_dp, n_tp),
        out_shape=jax.ShapeDtypeStruct((requests, question_tokens, width), bf16),
        in_specs=[smem, smem] + [hbm] * 7,
        out_specs=vmem,
        scratch_shapes=[
            pltpu.VMEM((question_tokens, width), bf16),
            pltpu.VMEM((held, tokens, width), bf16),
            pltpu.VMEM((1, n_tp * width), f32),
            pltpu.VMEM((8, 128), jnp.int32),
            pltpu.VMEM((n_dp, 8, 128), jnp.int32),
            pltpu.SMEM((n_dp, 8, 128), jnp.int32),
            pltpu.SMEM((requests,), jnp.int32),
            pltpu.VMEM((PIECES - 1, n_dp, SLOTS, piece, width), bf16),
            pltpu.VMEM((held, piece, 2 * heads_width), bf16),
            pltpu.VMEM((n_dp, SLOTS, piece, 2 * heads_width), bf16),
            pltpu.VMEM((n_dp * SLOTS, piece, 2 * heads_width), bf16),
            pltpu.VMEM((n_dp * SLOTS, piece, width), bf16),
            pltpu.VMEM((n_dp * SLOTS, piece, width), bf16),
            pltpu.VMEM((n_dp * SLOTS, piece, width), bf16),
            pltpu.VMEM((PIECES, n_tp, rows, width), bf16),
            pltpu.VMEM((n_tp, question_tokens, width), bf16),
            pltpu.VMEM((n_tp, width, heads_width), bf16),
            pltpu.VMEM((n_tp, width, 2 * heads_width), bf16),
            pltpu.VMEM((heads_width, n_tp * width), bf16),
            pltpu.VMEM((requests, question_tokens, heads_width), bf16),
            pltpu.VMEM((2, 2, SIDE, part_half, width), bf16),
            pltpu.VMEM((2, 2, SIDE, part_half, width), bf16),
            pltpu.VMEM((2, 2, SIDE, part_rows, width), bf16),
            pltpu.VMEM((2, 2, SIDE, part_rows, width), bf16),
            pltpu.VMEM((2, SIDE, part_rows, width), f32),
            pltpu.VMEM((2, 2, part_half, width), bf16),
            pltpu.VMEM((2, 2, part_half, width), bf16),
            pltpu.VMEM((2, 2, part_rows, width), bf16),
            pltpu.VMEM((2, 2, part_rows, width), bf16),
            pltpu.VMEM((rows, 2 * heads_width), f32),
            pltpu.VMEM((rows, 128), f32),
            pltpu.VMEM((question_tokens, 3 * heads_width), f32),
            pltpu.VMEM((question_tokens, 128), f32),
            pltpu.VMEM((requests, tokens, heads_width), bf16),
            pltpu.VMEM((requests, tokens, heads_width), bf16),
            sem((4,)),
            sem((3,)),
            sem,
            sem((n_dp,)),
            sem((n_dp,)),
            sem((6,)),
            sem((6,)),
            sem((PIECES, n_dp)),
            sem((PIECES, n_dp)),
            sem((n_dp,)),
            sem((n_dp,)),
            sem((PIECES, 40)),
            sem((PIECES, 40)),
            sem((40,)),
            sem((40,)),
        ],
        compiler_params=pltpu.CompilerParams(
            collective_id=0, has_side_effects=True, vmem_limit_bytes=56 * 1024 * 1024
        ),
        name="attention_sublayer",
    )(
        retrieved,
        location,
        questions.reshape(question_tokens, width),
        memory,
        norm_gain.reshape(1, n_tp * width),
        w_query.reshape(n_tp, width, heads_width),
        w_key.reshape(n_tp, width, heads_width),
        w_value.reshape(n_tp, width, heads_width),
        w_out,
    )
    return updated[None]


def solution(mesh):
    placed = (
        P("dp", None, "tensor"),
        P("dp", None, "tensor"),
        P("dp", None),
        P(),
        P(),
        P(None, "tensor"),
        P(None, "tensor"),
        P(None, "tensor"),
        P("tensor", None),
    )
    return jax.shard_map(
        on_device,
        mesh=mesh,
        in_specs=placed,
        out_specs=P("dp", None, None, "tensor"),
        check_vma=False,
    )
```
